32 devices in a mesh: dom: 8 (over z, x), sub: 4 (over y, core).
Axes of the slice: x: 2, y: 2, z: 4, core: 2. Of those that a mesh axis runs over, the one named last changes fastest.
Arguments:
- initial_state: float32 [320, 8192], P(None, ('dom', 'sub')), may hold values from -6 to 6
- cotangent: float32 [320, 8192], P(None, ('dom', 'sub')), may hold values from -6 to 6
- volume_operator: bfloat16 [320, 320], replicated, may hold values from -0.3125 to 0.3125
- in_weight: bfloat16 [64, 10], replicated, may hold values from -2 to 2
- in_bias: float32 [64], replicated, may hold values from -3 to 3
- mid_weight: bfloat16 [64, 64], replicated, may hold values from -0.75 to 0.75
- mid_bias: float32 [64], replicated, may hold values from -3 to 3
- out_weight: bfloat16 [5, 64], replicated, may hold values from -0.75 to 0.75
- flux_matrix: float32 [5, 5], replicated, may hold values from -2.5 to 2.5
- dom_send: int32 [8, 1024], P('dom', 'sub'), may hold values from 0 to 1535
- dom_count: int32 [8, 32], P('dom', 'sub'), may hold values from 0 to 32, as said below
- sub_send: int32 [8, 2048], P('dom', 'sub'), may hold values from 0 to 1535
- partner: int32 [8, 6144], P('dom', 'sub'), may hold values from 0 to 2303, as said below
Outputs:
- final_state: float32 [320, 8192], P(None, ('dom', 'sub'))
- adjoint_state: float32 [320, 8192], P(None, ('dom', 'sub'))
The draws below stay inside these ranges and needn't reach their ends.
Inputs may be any that keep to these rules, and one draw needn't show every extreme that they name: `dom_send`: local face slots, face*256+element. `dom_count`: counts of live slots; in every partition some block is full. `sub_send`: local face slots, face*256+element. `partner`: entries below 1536 name a local face slot; each received slot 6*256+r is named by exactly one face of the partition.
All inputs are finite; a program needn't handle non-finite values.
Results may differ from the reference program's by a relative error of at most 0.0033.
Values may be sent and summed in bfloat16 or wider, within the bound.
A program may use at most 64 MiB of HBM per device.

```python
import jax
import jax.numpy as jnp
import numpy as np
from jax import lax

VARS = 5
HIDDEN_SIZE = 64
REACH = 4
PEER_SLOTS = 32
SUB_SLOTS = 128
E_DEV = 256
ROWS = 320
ELEMS = 8192
SOURCES = 768
N_DOM = 8
N_SUB = 4


def draw_dom_count(key, part):
    devices = N_DOM * N_SUB
    pair_count = 2 * REACH
    key_one, key_two, key_three = jax.random.split(jax.random.fold_in(key, 11), 3)
    load_level = jax.random.randint(key_one, (devices, 1), 1, 5)
    counts = jax.random.randint(key_two, (devices, pair_count), PEER_SLOTS * load_level // 8, PEER_SLOTS * load_level // 4 + 1)
    chosen = jax.random.randint(key_three, (devices, 1), 0, pair_count)
    counts = jnp.where(jnp.arange(pair_count)[None, :] == chosen, PEER_SLOTS, counts)
    return counts.reshape(N_DOM, N_SUB * pair_count).astype(jnp.int32)


def draw_partner(key, part):
    devices = N_DOM * N_SUB
    faces = 6 * E_DEV
    device_keys = jax.random.split(jax.random.fold_in(key, 37), devices)

    def one_device(device_key):
        key_one, key_two = jax.random.split(device_key, 2)
        shuffle = jax.random.permutation(key_one, faces)
        values = jnp.concatenate([faces + jnp.arange(SOURCES), jax.random.randint(key_two, (faces - SOURCES,), 0, faces)])
        return values[jnp.argsort(shuffle)]
    partner_table = jax.vmap(one_device)(device_keys)
    return partner_table.reshape(N_DOM, N_SUB * faces).astype(jnp.int32)


def place_ends(result, rng, smallest, high):
    extent = result.shape
    spot = [jax.random.randint(jax.random.fold_in(rng, axis), (), 0, extent[axis]) for axis in range(len(extent))]
    result = result.at[tuple(spot)].set(smallest)
    longest = extent.index(max(extent))
    spot[longest] = (spot[longest] + 1) % extent[longest]
    return result.at[tuple(spot)].set(high)


def steps_of(key, shape, cuts, smallest, largest):
    factor_of = 1.0
    for axis_at, shards_of in cuts:
        draws = jax.random.uniform(jax.random.fold_in(jax.random.fold_in(key, 6), axis_at), (shards_of,), jnp.float32, smallest / len(cuts), largest / len(cuts))
        factor_of = factor_of * jnp.repeat(jnp.exp(draws), shape[axis_at] // shards_of).reshape((-1,) + (1,) * (len(shape) - 1 - axis_at))
    return factor_of


def noise(stream_key, shape, deviation, most, cuts=(), held_as=jnp.bfloat16):
    result = deviation * jax.random.normal(stream_key, shape, jnp.float32)
    if cuts:
        result = result * steps_of(stream_key, shape, cuts, -0.22, 0.18)
    return jnp.clip(result, -most, most).astype(held_as)


def setup_inputs(seed: int = 0) -> dict:
    splits = jax.random.split(jax.random.key(seed), 14)
    initial_state = noise(splits[0], (ROWS, ELEMS), 1.0, 6.0, ((1, 32),), jnp.float32)
    cotangent = noise(splits[1], (ROWS, ELEMS), 1.0, 6.0, ((1, 32),), jnp.float32)
    volume_operator = noise(splits[2], (ROWS, ROWS), ROWS ** -0.5, 0.3125)
    in_weight = noise(splits[3], (HIDDEN_SIZE, 2 * VARS), (2 * VARS) ** -0.5, 2.0)
    in_bias = noise(splits[4], (HIDDEN_SIZE,), 0.5, 3.0, (), jnp.float32)
    mid_weight = noise(splits[5], (HIDDEN_SIZE, HIDDEN_SIZE), HIDDEN_SIZE ** -0.5, 0.75)
    mid_bias = noise(splits[6], (HIDDEN_SIZE,), 0.5, 3.0, (), jnp.float32)
    out_weight = noise(splits[7], (VARS, HIDDEN_SIZE), HIDDEN_SIZE ** -0.5, 0.75)
    flux_matrix = noise(splits[8], (VARS, VARS), VARS ** -0.5, 2.5, (), jnp.float32)
    dom_send = place_ends(jax.random.randint(splits[9], (N_DOM, N_SUB * 2 * REACH * PEER_SLOTS), 0, 6 * E_DEV), jax.random.fold_in(splits[9], 1), 0, (6 * E_DEV) - 1).astype(jnp.int32)
    dom_count = draw_dom_count(jax.random.fold_in(splits[13], 71), 0)
    sub_send = place_ends(jax.random.randint(splits[11], (N_DOM, N_SUB * N_SUB * SUB_SLOTS), 0, 6 * E_DEV), jax.random.fold_in(splits[11], 1), 0, (6 * E_DEV) - 1).astype(jnp.int32)
    partner = draw_partner(jax.random.fold_in(splits[13], 71), 0)
    return dict(initial_state=initial_state, cotangent=cotangent, volume_operator=volume_operator, in_weight=in_weight, in_bias=in_bias, mid_weight=mid_weight, mid_bias=mid_bias, out_weight=out_weight, flux_matrix=flux_matrix, dom_send=dom_send, dom_count=dom_count, sub_send=sub_send, partner=partner)


time_step = 0.4
lift_gain = 1.5


def face_traces(values):
    elements = values.shape[-1]
    element_cube = values.reshape(5, 4, 4, 4, elements)
    face_blocks = [element_cube[:, :, :, 0, :], element_cube[:, :, :, 3, :], element_cube[:, :, 0, :, :], element_cube[:, :, 3, :, :], element_cube[:, 0, :, :, :], element_cube[:, 3, :, :, :]]
    stacked = jnp.stack([face_block.reshape(5, 16, elements) for face_block in face_blocks], axis=2)
    return stacked.reshape(80, 6 * elements)


def lift_traces(faces):
    elements = faces.shape[-1] // 6
    pieces = faces.reshape(5, 4, 4, 6, elements)
    element_cube = jnp.zeros((5, 4, 4, 4, elements), faces.dtype)
    element_cube = element_cube.at[:, :, :, 0, :].add(pieces[:, :, :, 0, :])
    element_cube = element_cube.at[:, :, :, 3, :].add(pieces[:, :, :, 1, :])
    element_cube = element_cube.at[:, :, 0, :, :].add(pieces[:, :, :, 2, :])
    element_cube = element_cube.at[:, :, 3, :, :].add(pieces[:, :, :, 3, :])
    element_cube = element_cube.at[:, 0, :, :, :].add(pieces[:, :, :, 4, :])
    element_cube = element_cube.at[:, 3, :, :, :].add(pieces[:, :, :, 5, :])
    return element_cube.reshape(320, elements)


def node_groups(values):
    elements = values.shape[-1]
    return jnp.moveaxis(values.reshape(values.shape[0] // 64, 8, 8 * elements), 1, 0)


def ungroup(blocks):
    return jnp.moveaxis(blocks, 0, 1).reshape(blocks.shape[1] * 64, blocks.shape[2] // 8)


def closure_net(field_b, volume_b, weights):
    in_weight, in_bias, mid_weight, mid_bias, out_weight = weights

    def one_block(members):
        inputs = jnp.concatenate(members, axis=0)
        first_act = jnp.tanh(jnp.dot(in_weight, inputs, preferred_element_type=jnp.float32) + in_bias[:, None]).astype(jnp.bfloat16)
        second_act = jnp.tanh(jnp.dot(mid_weight, first_act, preferred_element_type=jnp.float32) + mid_bias[:, None]).astype(jnp.bfloat16)
        return jnp.dot(out_weight, second_act, preferred_element_type=jnp.float32)

    return ungroup(lax.map(one_block, (node_groups(field_b), node_groups(volume_b))))


def closure_back(field_b, volume_b, upstream, weights):
    in_weight, in_bias, mid_weight, mid_bias, out_weight = weights

    def one_block(members):
        field_part, volume_part, upstream_part = members
        inputs = jnp.concatenate([field_part, volume_part], axis=0)
        first_act = jnp.tanh(jnp.dot(in_weight, inputs, preferred_element_type=jnp.float32) + in_bias[:, None])
        second_act = jnp.tanh(jnp.dot(mid_weight, first_act.astype(jnp.bfloat16), preferred_element_type=jnp.float32) + mid_bias[:, None])
        second_delta = (jnp.dot(out_weight.T, upstream_part.astype(jnp.bfloat16), preferred_element_type=jnp.float32) * (1.0 - second_act * second_act)).astype(jnp.bfloat16)
        first_delta = (jnp.dot(mid_weight.T, second_delta, preferred_element_type=jnp.float32) * (1.0 - first_act * first_act)).astype(jnp.bfloat16)
        return jnp.dot(in_weight.T, first_delta, preferred_element_type=jnp.float32)

    backward = ungroup(lax.map(one_block, (node_groups(field_b), node_groups(volume_b), node_groups(upstream))))
    return backward[:320], backward[320:]


def volume_terms(values, volume_operator, weights):
    field_b = values.astype(jnp.bfloat16)
    volume = jnp.dot(volume_operator, field_b, preferred_element_type=jnp.float32)
    closure = closure_net(field_b, volume.astype(jnp.bfloat16), weights)
    return volume + closure, face_traces(field_b)


def face_flux(traces, neighbours, flux_matrix):
    jump = neighbours.astype(jnp.float32) - traces.astype(jnp.float32)
    flux = jnp.dot(flux_matrix, jump.reshape(5, -1), precision=lax.Precision.HIGHEST).reshape(80, -1)
    return lift_gain * lift_traces(flux)


def faces_adjoint(adjoint, face_links, flux_matrix, source_total):
    face_grad = lift_gain * face_traces(adjoint)
    jump_grad = jnp.dot(flux_matrix.T, face_grad.reshape(5, -1), precision=lax.Precision.HIGHEST).reshape(80, -1)
    source_grad = jnp.zeros((80, source_total), jnp.float32).at[:, face_links].add(jump_grad)
    return jump_grad, source_grad


def rest_adjoint(values, adjoint, jump_grad, local_grad, dom_returned, sub_returned, dom_lists, sub_lists, volume_operator, weights):
    field_b = values.astype(jnp.bfloat16)
    volume_b = jnp.dot(volume_operator, field_b, preferred_element_type=jnp.float32).astype(jnp.bfloat16)
    trace_grad = (local_grad - jump_grad).at[:, dom_lists].add(dom_returned).at[:, sub_lists].add(sub_returned)
    field_grad, volume_grad = closure_back(field_b, volume_b, adjoint, weights)
    volume_total = (adjoint + volume_grad).astype(jnp.bfloat16)
    return jnp.dot(volume_operator.T, volume_total, preferred_element_type=jnp.float32) + field_grad + lift_traces(trace_grad)


def take_columns(table, columns):
    return jnp.take(table, columns, axis=1)


def reference(initial_state, cotangent, volume_operator, in_weight, in_bias, mid_weight, mid_bias, out_weight, flux_matrix, dom_send, dom_count, sub_send, partner):
    devices = N_DOM * N_SUB
    elements = E_DEV
    pair_count = 2 * REACH
    offsets = jnp.array(np.array([offset for offset in range(-REACH, REACH + 1) if offset != 0], dtype=np.int32))
    weights = (in_weight, in_bias, mid_weight, mid_bias, out_weight)
    dom_lists = dom_send.reshape(devices, pair_count * PEER_SLOTS)
    dom_mask = jnp.arange(PEER_SLOTS, dtype=jnp.int32)[None, None, :] < dom_count.reshape(devices, pair_count)[:, :, None]
    sub_lists = sub_send.reshape(devices, N_SUB * SUB_SLOTS)
    face_links = partner.reshape(devices, 6 * elements)
    source_total = 6 * elements + pair_count * PEER_SLOTS + N_SUB * SUB_SLOTS

    def split_rows(values):
        return values.reshape(320, devices, elements).transpose(1, 0, 2)

    def join_rows(values):
        return values.transpose(1, 0, 2).reshape(320, devices * elements)

    def route_dom(values, direction):
        layout = values.reshape(N_DOM, N_SUB, 80, pair_count, PEER_SLOTS)
        anchor = jnp.arange(N_DOM, dtype=jnp.int32)[:, None] - direction * offsets[None, :]
        inside = (anchor >= 0) & (anchor < N_DOM)
        picked = layout[jnp.clip(anchor, 0, N_DOM - 1), :, :, jnp.arange(pair_count, dtype=jnp.int32)[None, :], :]
        picked = jnp.where(inside[:, :, None, None, None], picked, jnp.zeros_like(picked))
        return picked.transpose(0, 2, 3, 1, 4).reshape(devices, 80, pair_count, PEER_SLOTS)

    def route_sub(values):
        layout = values.reshape(N_DOM, N_SUB, 80, N_SUB, SUB_SLOTS)
        return layout.transpose(0, 3, 2, 1, 4).reshape(devices, 80, N_SUB, SUB_SLOTS)

    def residual(fields):
        def local_front(values):
            return volume_terms(values, volume_operator, weights)

        base, traces = lax.map(local_front, fields)
        dom_sent = jax.vmap(take_columns)(traces, dom_lists).reshape(devices, 80, pair_count, PEER_SLOTS)
        dom_sent = jnp.where(dom_mask[:, None], dom_sent, jnp.zeros_like(dom_sent))
        sub_sent = jax.vmap(take_columns)(traces, sub_lists).reshape(devices, 80, N_SUB, SUB_SLOTS)
        dom_received = route_dom(dom_sent, 1).reshape(devices, 80, -1)
        sub_received = route_sub(sub_sent).reshape(devices, 80, -1)

        def local_back(members):
            base_part, trace_part, dom_part, sub_part, link_part = members
            sources = jnp.concatenate([trace_part, dom_part, sub_part], axis=1)
            return base_part + face_flux(trace_part, jnp.take(sources, link_part, axis=1), flux_matrix)

        return lax.map(local_back, (base, traces, dom_received, sub_received, face_links))

    def adjoint_of(fields, adjoints):
        def local_faces(members):
            return faces_adjoint(members[0], members[1], flux_matrix, source_total)

        jump_grad, source_grad = lax.map(local_faces, (adjoints, face_links))
        local_grad = source_grad[:, :, :6 * elements]
        dom_grad = source_grad[:, :, 6 * elements:6 * elements + pair_count * PEER_SLOTS].reshape(devices, 80, pair_count, PEER_SLOTS)
        sub_grad = source_grad[:, :, 6 * elements + pair_count * PEER_SLOTS:].reshape(devices, 80, N_SUB, SUB_SLOTS)
        dom_back = route_dom(dom_grad, -1)
        dom_returned = jnp.where(dom_mask[:, None], dom_back, jnp.zeros_like(dom_back)).reshape(devices, 80, -1)
        sub_returned = route_sub(sub_grad).reshape(devices, 80, -1)

        def local_rest(members):
            values, adjoint, jump_part, local_part, dom_part, sub_part, dom_part_lists, sub_part_lists = members
            return rest_adjoint(values, adjoint, jump_part, local_part, dom_part, sub_part, dom_part_lists, sub_part_lists, volume_operator, weights)

        return lax.map(local_rest, (fields, adjoints, jump_grad, local_grad, dom_returned, sub_returned, dom_lists, sub_lists))

    start_field = split_rows(initial_state)
    middle_field = start_field + time_step * residual(start_field)
    final_field = 0.5 * start_field + 0.5 * (middle_field + time_step * residual(middle_field))
    adjoint_final = split_rows(cotangent)
    adjoint_middle = 0.5 * adjoint_final + 0.5 * time_step * adjoint_of(middle_field, adjoint_final)
    adjoint_start = 0.5 * adjoint_final + adjoint_middle + time_step * adjoint_of(start_field, adjoint_middle)
    return join_rows(final_field), join_rows(adjoint_start)
```

```python
import functools

import jax
import jax.numpy as jnp
import numpy as np
from jax import lax
from jax.experimental import pallas as pl
from jax.experimental.pallas import tpu as pltpu
from jax.sharding import PartitionSpec as P

REACH = 4
OFFSETS = [offset for offset in range(-REACH, REACH + 1) if offset != 0]
PAIRS = len(OFFSETS)
MESH = pl.DeviceIdType.MESH

time_step = 0.4
lift_gain = 1.5
BF = jnp.bfloat16
F32 = jnp.float32


def face_rows():
    table = np.zeros((6, 5, 16, 5, 64), np.float32)
    for k in range(16):
        low, high = k % 4, k // 4
        nodes = [
            4 * k,
            3 + 4 * k,
            low + 16 * high,
            low + 12 + 16 * high,
            k,
            k + 48,
        ]
        for f, node in enumerate(nodes):
            for v in range(5):
                table[f, v, k, v, node] = 1.0
    return table.reshape(480, 320)


def mm(a, b):
    return jnp.dot(a, b, preferred_element_type=F32)


def mm_nt(a, b):
    return lax.dot_general(a, b, (((1,), (1,)), ((), ())), preferred_element_type=F32)


def mm_tn(a, b):
    return lax.dot_general(a, b, (((0,), (0,)), ((), ())), preferred_element_type=F32)


def split(values):
    high = values.astype(BF)
    return high, (values - high.astype(F32)).astype(BF)


def to_wide(faces, elements):
    return jnp.concatenate([faces[f * 80 : (f + 1) * 80] for f in range(6)], axis=1)


def to_tall(wide, elements):
    return jnp.concatenate(
        [wide[:, f * elements : (f + 1) * elements] for f in range(6)], axis=0
    )


def lift(face_t, wide, elements):
    high, low = split(to_tall(wide, elements))
    return mm(face_t, high) + mm(face_t, low)


def mix(flux_ref, values, transposed):
    rows = []
    for v in range(5):
        total = None
        for u in range(5):
            weight = flux_ref[u, v] if transposed else flux_ref[v, u]
            term = weight * values[u * 16 : (u + 1) * 16]
            total = term if total is None else total + term
        rows.append(total)
    return jnp.concatenate(rows, axis=0)


def one_hot_rows(row_list, base, rows):
    width = row_list.shape[1]
    shifted = (row_list - base).astype(F32)
    wide = jnp.broadcast_to(shifted, (rows, width))
    spot = lax.broadcasted_iota(jnp.int32, (rows, width), 0).astype(F32)
    return jnp.where(wide == spot, 1.0, 0.0).astype(BF)


def kernel(
    n_dom,
    n_sub,
    w_ref,
    ct_ref,
    vol_op_ref,
    in_w_ref,
    in_b_ref,
    mid_w_ref,
    mid_b_ref,
    out_w_ref,
    flux_ref,
    dom_ref,
    count_ref,
    sub_ref,
    partner_ref,
    face_ref,
    face_t_ref,
    final_ref,
    adj_ref,
    pick,
    send_hot,
    w1,
    w1t,
    m4,
    m4t,
    o16,
    o16t,
    bias1,
    bias2,
    x_in,
    g_in,
    clo,
    x_grad,
    slope1,
    slope2,
    traces_s,
    near,
    grad_near,
    middle_s,
    adj_mid_s,
    out_buf,
    in_buf,
    dom_send_sem,
    dom_recv_sem,
    sub_send_sem,
    sub_recv_sem,
):
    elements = w_ref.shape[1]
    faces = 6 * elements
    dom_width = dom_ref.shape[1]
    peer_slots = dom_width // PAIRS
    sub_width = sub_ref.shape[1]
    sub_slots = sub_width // n_sub
    slots = dom_width + sub_width
    d = lax.axis_index("dom")
    s = lax.axis_index("sub")

    def inside(j):
        target = d + OFFSETS[j]
        return (target >= 0) & (target < n_dom)

    barrier = pltpu.get_barrier_semaphore()
    expected = n_sub - 1
    for j in range(PAIRS):
        expected = expected + jnp.where(inside(j), 1, 0)

        @pl.when(inside(j))
        def _():
            pl.semaphore_signal(
                barrier, inc=1, device_id=(d + OFFSETS[j], s), device_id_type=MESH
            )

    for step in range(1, n_sub):
        pl.semaphore_signal(
            barrier, inc=1, device_id=(d, lax.rem(s + step, n_sub)), device_id_type=MESH
        )

    def dom_copy(phase, j):
        rows = pl.ds(j * peer_slots, peer_slots)
        return pltpu.make_async_remote_copy(
            src_ref=out_buf.at[phase, rows],
            dst_ref=in_buf.at[phase, rows],
            send_sem=dom_send_sem.at[phase, j],
            recv_sem=dom_recv_sem.at[phase, j],
            device_id=(d + OFFSETS[j], s),
            device_id_type=MESH,
        )

    def sub_copy(phase, step):
        there = lax.rem(s + step, n_sub)
        source = pl.ds(pl.multiple_of(dom_width + there * sub_slots, 32), sub_slots)
        target = pl.ds(pl.multiple_of(dom_width + s * sub_slots, 32), sub_slots)
        return pltpu.make_async_remote_copy(
            src_ref=out_buf.at[phase, source],
            dst_ref=in_buf.at[phase, target],
            send_sem=sub_send_sem.at[phase, step - 1],
            recv_sem=sub_recv_sem.at[phase, step - 1],
            device_id=(d, there),
            device_id_type=MESH,
        )

    def start_exchange(phase):
        for j in range(PAIRS):

            @pl.when(inside(j))
            def _():
                dom_copy(phase, j).start()

        for step in range(1, n_sub):
            sub_copy(phase, step).start()
        own = pl.ds(pl.multiple_of(dom_width + s * sub_slots, 32), sub_slots)
        in_buf[phase, own, :] = out_buf[phase, own, :]

    def wait_exchange(phase):
        for j in range(PAIRS):
            @pl.when(inside(PAIRS - 1 - j))
            def _():
                dom_copy(phase, j).wait_recv()

            @pl.when(inside(j))
            def _():
                dom_copy(phase, j).wait_send()

            @pl.when(jnp.logical_not(inside(PAIRS - 1 - j)))
            def _():
                in_buf[phase, pl.ds(j * peer_slots, peer_slots), :] = jnp.zeros(
                    (peer_slots, 256), BF
                )

        for step in range(1, n_sub):
            sub_copy(phase, step).wait()

    def flip(rows):
        parts = [
            rows[j * peer_slots : (j + 1) * peer_slots] for j in reversed(range(PAIRS))
        ]
        return jnp.concatenate(parts + [rows[dom_width:]], axis=0)

    def slots_to_rows(values):
        padded = jnp.concatenate([values, jnp.zeros((48, slots), F32)], axis=0)
        return jnp.transpose(padded)

    def put_forward(phase, values):
        out_buf[phase, :, 0:128] = slots_to_rows(values).astype(BF)

    def put_backward(phase, values):
        out_buf[phase, :, 128:256] = flip(slots_to_rows(values)).astype(BF)

    def got_forward(phase):
        return jnp.transpose(in_buf[phase, :, 0:128].astype(F32))[:80].astype(BF)

    def got_backward(phase):
        rows = flip(in_buf[phase, :, 128:256].astype(F32))
        return jnp.transpose(rows)[:80].astype(BF)

    lane = lax.broadcasted_iota(jnp.int32, (1, dom_width), 1)
    dom_list = dom_ref[...]
    for j in range(PAIRS):
        dead = (lane >= j * peer_slots + count_ref[0, j]) & (lane < (j + 1) * peer_slots)
        dom_list = jnp.where(dead, -1, dom_list)
    send_list = jnp.concatenate([dom_list, sub_ref[...]], axis=1)
    for base in range(0, faces, 256):
        send_hot[pl.ds(base, 256), :] = one_hot_rows(send_list, base, 256)
    partner = partner_ref[...]
    for base in range(faces, faces + slots, 256):
        pick[pl.ds(base, 256), :] = one_hot_rows(partner, base, 256)

    face = face_ref[...]
    face_t = face_t_ref[...]

    def traces_of(field_b):
        return to_wide(mm(face, field_b), elements).astype(BF)

    def jump_grad_of(g):
        high, low = split(g)
        values = to_wide(mm(face, high) + mm(face, low), elements)
        return mix(flux_ref, lift_gain * values, True)

    pick_near = pick.at[pl.ds(0, faces)]
    pick_far = pick.at[pl.ds(faces, slots)]

    field0 = w_ref[...].astype(BF)
    traces0 = traces_of(field0)
    put_forward(0, mm(traces0, send_hot[...]))
    jump0 = jump_grad_of(ct_ref[...])
    jump0_b = jump0.astype(BF)
    put_backward(0, mm_nt(jump0_b, pick_far[...]))
    pl.semaphore_wait(barrier, expected)
    start_exchange(0)

    for base in range(0, faces, 256):
        pick[pl.ds(base, 256), :] = one_hot_rows(partner, base, 256)
    near[...] = mm(traces0, pick_near[...]) - traces0.astype(F32)
    grad_near[...] = mm_nt(jump0_b, pick_near[...]) - jump0

    def iota(shape, axis):
        return lax.broadcasted_iota(jnp.int32, shape, axis)

    def hot(mask):
        return jnp.where(mask, 1.0, 0.0).astype(BF)

    e1 = hot(iota((1024, 64), 0) % 64 == iota((1024, 64), 1))
    e1t = hot(iota((64, 1024), 1) % 64 == iota((64, 1024), 0))
    e2 = hot(iota((10, 160), 1) // 16 == iota((10, 160), 0))
    e2t = hot(iota((160, 10), 0) // 16 == iota((160, 10), 1))
    e3 = hot(iota((5, 80), 1) // 16 == iota((5, 80), 0))
    e3t = hot(iota((80, 5), 0) // 16 == iota((80, 5), 1))
    in_w, mid_w, out_w = in_w_ref[...], mid_w_ref[...], out_w_ref[...]

    def masked(values, mask):
        return jnp.where(mask, values, 0.0).astype(BF)

    w1[...] = masked(
        mm(mm(e1, in_w).astype(BF), e2),
        iota((1024, 160), 0) // 64 == iota((1024, 160), 1) % 16,
    )
    w1t[...] = masked(
        mm(mm_nt(e2t, in_w).astype(BF), e1t),
        iota((160, 1024), 1) // 64 == iota((160, 1024), 0) % 16,
    )
    o16[...] = masked(
        mm(mm(e3t, out_w).astype(BF), e1t),
        iota((80, 1024), 1) // 64 == iota((80, 1024), 0) % 16,
    )
    o16t[...] = masked(
        mm(mm_nt(e1, out_w).astype(BF), e3),
        iota((1024, 80), 0) // 64 == iota((1024, 80), 1) % 16,
    )
    same = iota((256, 256), 0) // 64 == iota((256, 256), 1) // 64
    m4[...] = masked(mm(mm(e1[:256], mid_w).astype(BF), e1t[:, :256]), same)
    m4t[...] = masked(mm(mm_nt(e1[:256], mid_w).astype(BF), e1t[:, :256]), same)
    diag = iota((256, 64), 0) % 64 == iota((256, 64), 1)
    for bias_ref, target in ((in_b_ref, bias1), (mid_b_ref, bias2)):
        column = jnp.sum(jnp.where(diag, bias_ref[...], 0.0), axis=1, keepdims=True)
        target[...] = jnp.broadcast_to(column, target.shape)

    def activations(x, sub):
        h1 = jnp.tanh(mm(w1[pl.ds(sub * 256, 256), :], x) + bias1[...])
        h2 = jnp.tanh(mm(m4[...], h1.astype(BF)) + bias2[...])
        return h1, h2

    def back(upstream, sub, factor1, factor2):
        d2 = (mm(o16t[pl.ds(sub * 256, 256), :], upstream) * factor2).astype(BF)
        d1 = (mm(m4t[...], d2) * factor1).astype(BF)
        return mm(w1t[:, pl.ds(sub * 256, 256)], d1)

    def nodes_of(g):
        return pl.ds(pl.multiple_of(g * 16, 16), 16)

    def set_inputs(field_b, volume_b):
        x_in[0:5] = field_b.reshape(5, 64, elements)
        x_in[5:10] = volume_b.reshape(5, 64, elements)

    volume0 = mm(vol_op_ref[...], field0)
    set_inputs(field0, volume0.astype(BF))

    def forward_group(g, carry):
        x = x_in[:, nodes_of(g), :].reshape(160, elements)
        total = jnp.zeros((80, elements), F32)
        for sub in range(4):
            h1, h2 = activations(x, sub)
            rows = pl.ds(pl.multiple_of(g * 1024 + sub * 256, 256), 256)
            slope1[rows, :] = (1.0 - h1 * h1).astype(BF)
            slope2[rows, :] = (1.0 - h2 * h2).astype(BF)
            total = total + mm(o16[:, pl.ds(sub * 256, 256)], h2.astype(BF))
        clo[:, nodes_of(g), :] = total.reshape(5, 16, elements)
        return carry

    lax.fori_loop(0, 4, forward_group, 0)
    base0 = w_ref[...] + time_step * (volume0 + clo[...].reshape(320, elements))

    wait_exchange(0)
    jump = near[...] + mm(got_forward(0), pick_far[...])
    flux = mix(flux_ref, lift_gain * jump, False)
    middle = base0 + time_step * lift(face_t, flux, elements)
    middle_s[...] = middle
    trace_grad = grad_near[...] + mm_nt(got_backward(0), send_hot[...])
    adj_lift = lift(face_t, trace_grad, elements)

    field1 = middle.astype(BF)
    traces1 = traces_of(field1)
    traces_s[...] = traces1
    put_forward(1, mm(traces1, send_hot[...]))
    volume1 = mm(vol_op_ref[...], field1)
    set_inputs(field1, volume1.astype(BF))
    g_in[...] = ct_ref[...].astype(BF).reshape(5, 64, elements)

    def both_group(g, carry):
        x = x_in[:, nodes_of(g), :].reshape(160, elements)
        upstream = g_in[:, nodes_of(g), :].reshape(80, elements)
        total = jnp.zeros((80, elements), F32)
        grads = jnp.zeros((160, elements), F32)
        for sub in range(4):
            h1, h2 = activations(x, sub)
            total = total + mm(o16[:, pl.ds(sub * 256, 256)], h2.astype(BF))
            grads = grads + back(upstream, sub, 1.0 - h1 * h1, 1.0 - h2 * h2)
        clo[:, nodes_of(g), :] = total.reshape(5, 16, elements)
        x_grad[:, nodes_of(g), :] = grads.reshape(10, 16, elements)
        return carry

    lax.fori_loop(0, 4, both_group, 0)

    def input_part(adjoint):
        field_grad = x_grad[0:5].reshape(320, elements)
        volume_grad = x_grad[5:10].reshape(320, elements)
        return mm_tn(vol_op_ref[...], (adjoint + volume_grad).astype(BF)) + field_grad

    ct = ct_ref[...]
    adj_mid = 0.5 * ct + 0.5 * time_step * (input_part(ct) + adj_lift)
    adj_mid_s[...] = adj_mid
    jump1 = jump_grad_of(adj_mid)
    jump1_b = jump1.astype(BF)
    put_backward(1, mm_nt(jump1_b, pick_far[...]))
    start_exchange(1)

    final_ref[...] = 0.5 * w_ref[...] + 0.5 * (
        middle_s[...] + time_step * (volume1 + clo[...].reshape(320, elements))
    )
    near[...] = mm(traces_s[...], pick_near[...]) - traces_s[...].astype(F32)
    grad_near[...] = mm_nt(jump1_b, pick_near[...]) - jump1
    g_in[...] = adj_mid.astype(BF).reshape(5, 64, elements)

    def back_group(g, carry):
        upstream = g_in[:, nodes_of(g), :].reshape(80, elements)
        grads = jnp.zeros((160, elements), F32)
        for sub in range(4):
            rows = pl.ds(pl.multiple_of(g * 1024 + sub * 256, 256), 256)
            grads = grads + back(
                upstream, sub, slope1[rows, :].astype(F32), slope2[rows, :].astype(F32)
            )
        x_grad[:, nodes_of(g), :] = grads.reshape(10, 16, elements)
        return carry

    lax.fori_loop(0, 4, back_group, 0)
    adj_mid = adj_mid_s[...]
    adj_ref[...] = 0.5 * ct_ref[...] + adj_mid + time_step * input_part(adj_mid)

    wait_exchange(1)
    jump = near[...] + mm(got_forward(1), pick_far[...])
    flux = mix(flux_ref, lift_gain * jump, False)
    final_ref[...] += 0.5 * time_step * lift(face_t, flux, elements)
    trace_grad = grad_near[...] + mm_nt(got_backward(1), send_hot[...])
    adj_ref[...] += time_step * lift(face_t, trace_grad, elements)


def body(
    n_dom,
    n_sub,
    initial_state,
    cotangent,
    volume_operator,
    in_weight,
    in_bias,
    mid_weight,
    mid_bias,
    out_weight,
    flux_matrix,
    dom_send,
    dom_count,
    sub_send,
    partner,
):
    elements = initial_state.shape[1]
    faces = 6 * elements
    slots = dom_send.shape[1] + sub_send.shape[1]
    table = face_rows()
    vmem = pl.BlockSpec(memory_space=pltpu.VMEM)
    smem = pl.BlockSpec(memory_space=pltpu.SMEM)
    state = jax.ShapeDtypeStruct(initial_state.shape, F32)
    return pl.pallas_call(
        functools.partial(kernel, n_dom, n_sub),
        out_shape=(state, state),
        in_specs=[vmem] * 8 + [smem, vmem, smem] + [vmem] * 4,
        out_specs=(vmem, vmem),
        scratch_shapes=[
            pltpu.VMEM((faces + slots, faces), BF),
            pltpu.VMEM((faces, slots), BF),
            pltpu.VMEM((1024, 160), BF),
            pltpu.VMEM((160, 1024), BF),
            pltpu.VMEM((256, 256), BF),
            pltpu.VMEM((256, 256), BF),
            pltpu.VMEM((80, 1024), BF),
            pltpu.VMEM((1024, 80), BF),
            pltpu.VMEM((256, elements), F32),
            pltpu.VMEM((256, elements), F32),
            pltpu.VMEM((10, 64, elements), BF),
            pltpu.VMEM((5, 64, elements), BF),
            pltpu.VMEM((5, 64, elements), F32),
            pltpu.VMEM((10, 64, elements), F32),
            pltpu.VMEM((4096, elements), BF),
            pltpu.VMEM((4096, elements), BF),
            pltpu.VMEM((80, faces), BF),
            pltpu.VMEM((80, faces), F32),
            pltpu.VMEM((80, faces), F32),
            pltpu.VMEM(initial_state.shape, F32),
            pltpu.VMEM(initial_state.shape, F32),
            pltpu.VMEM((2, slots, 256), BF),
            pltpu.VMEM((2, slots, 256), BF),
            pltpu.SemaphoreType.DMA((2, PAIRS)),
            pltpu.SemaphoreType.DMA((2, PAIRS)),
            pltpu.SemaphoreType.DMA((2, n_sub - 1)),
            pltpu.SemaphoreType.DMA((2, n_sub - 1)),
        ],
        compiler_params=pltpu.CompilerParams(
            collective_id=0, has_side_effects=True, vmem_limit_bytes=56 * 1024 * 1024
        ),
        cost_estimate=pl.CostEstimate(
            flops=8_000_000_000, bytes_accessed=4_000_000, transcendentals=4_000_000
        ),
    )(
        initial_state,
        cotangent,
        volume_operator,
        in_weight,
        in_bias.reshape(1, -1),
        mid_weight,
        mid_bias.reshape(1, -1),
        out_weight,
        flux_matrix,
        dom_send,
        dom_count,
        sub_send,
        partner,
        jnp.asarray(table, BF),
        jnp.asarray(table.T, BF),
    )


def solution(mesh):
    return jax.shard_map(
        functools.partial(body, mesh.shape["dom"], mesh.shape["sub"]),
        mesh=mesh,
        in_specs=(
            P(None, ("dom", "sub")),
            P(None, ("dom", "sub")),
            P(),
            P(),
            P(),
            P(),
            P(),
            P(),
            P(),
            P("dom", "sub"),
            P("dom", "sub"),
            P("dom", "sub"),
            P("dom", "sub"),
        ),
        out_specs=(P(None, ("dom", "sub")), P(None, ("dom", "sub"))),
        check_vma=False,
    )
```

```python
import functools

import jax
import jax.numpy as jnp
from jax import lax
from jax.experimental import pallas as pl
from jax.experimental.pallas import tpu as pltpu
from jax.sharding import PartitionSpec as P

REACH = 4
OFFSETS = [offset for offset in range(-REACH, REACH + 1) if offset != 0]
PAIRS = len(OFFSETS)
MESH = pl.DeviceIdType.MESH

time_step = 0.4
lift_gain = 1.5
BF = jnp.bfloat16
F32 = jnp.float32


def iota(shape, axis):
    return lax.broadcasted_iota(jnp.int32, shape, axis)


def hot(mask):
    return jnp.where(mask, 1.0, 0.0).astype(BF)


def face_node(row):
    f = sum((row >= 80 * i).astype(jnp.int32) for i in range(1, 6))
    within = row - 80 * f
    v, k = within >> 4, within & 15
    end = f & 1
    node = jnp.where(
        f < 2,
        3 * end + 4 * k,
        jnp.where(f < 4, (k & 3) + 16 * (k >> 2) + 12 * end, k + 48 * end),
    )
    return 64 * v + node


def mm(a, b):
    return jnp.dot(a, b, preferred_element_type=F32)


def mm_nt(a, b):
    return lax.dot_general(a, b, (((1,), (1,)), ((), ())), preferred_element_type=F32)


def mm_tn(a, b):
    return lax.dot_general(a, b, (((0,), (0,)), ((), ())), preferred_element_type=F32)


def split(values):
    high = values.astype(BF)
    return high, (values - high.astype(F32)).astype(BF)


def to_wide(faces, elements):
    return jnp.concatenate([faces[f * 80 : (f + 1) * 80] for f in range(6)], axis=1)


def to_tall(wide, elements):
    return jnp.concatenate(
        [wide[:, f * elements : (f + 1) * elements] for f in range(6)], axis=0
    )


def lift(face_t, wide, elements):
    high, low = split(to_tall(wide, elements))
    return mm(face_t, high) + mm(face_t, low)


def mix(flux_ref, values, transposed):
    rows = []
    for v in range(5):
        total = None
        for u in range(5):
            weight = flux_ref[u, v] if transposed else flux_ref[v, u]
            term = weight * values[u * 16 : (u + 1) * 16]
            total = term if total is None else total + term
        rows.append(total)
    return jnp.concatenate(rows, axis=0)


def one_hot_rows(row_list, base, rows):
    width = row_list.shape[1]
    shifted = (row_list - base).astype(F32)
    wide = jnp.broadcast_to(shifted, (rows, width))
    spot = lax.broadcasted_iota(jnp.int32, (rows, width), 0).astype(F32)
    return jnp.where(wide == spot, 1.0, 0.0).astype(BF)


def kernel(
    n_dom,
    n_sub,
    w_ref,
    ct_ref,
    vol_op_ref,
    in_wt_ref,
    in_b_ref,
    mid_w_ref,
    mid_b_ref,
    out_w_ref,
    flux_ref,
    dom_ref,
    count_ref,
    sub_ref,
    partner_ref,
    final_ref,
    adj_ref,
    pick,
    send_hot,
    w1,
    w1t,
    m4,
    m4t,
    o16,
    o16t,
    bias1,
    bias2,
    x_in,
    g_in,
    clo,
    x_grad,
    slope1,
    slope2,
    traces_s,
    near,
    grad_near,
    jump0_s,
    jump1_s,
    middle_s,
    adj_mid_s,
    out_buf,
    in_buf,
    dom_send_sem,
    dom_recv_sem,
    sub_send_sem,
    sub_recv_sem,
):
    elements = w_ref.shape[1]
    faces = 6 * elements
    dom_width = dom_ref.shape[1]
    peer_slots = dom_width // PAIRS
    sub_width = sub_ref.shape[1]
    sub_slots = sub_width // n_sub
    slots = dom_width + sub_width
    d = lax.axis_index("dom")
    s = lax.axis_index("sub")

    def inside(j):
        target = d + OFFSETS[j]
        return (target >= 0) & (target < n_dom)

    barrier = pltpu.get_barrier_semaphore()
    expected = n_sub - 1
    for j in range(PAIRS):
        expected = expected + jnp.where(inside(j), 1, 0)

        @pl.when(inside(j))
        def _():
            pl.semaphore_signal(
                barrier, inc=1, device_id=(d + OFFSETS[j], s), device_id_type=MESH
            )

    for step in range(1, n_sub):
        pl.semaphore_signal(
            barrier, inc=1, device_id=(d, lax.rem(s + step, n_sub)), device_id_type=MESH
        )

    def dom_copy(phase, j):
        rows = pl.ds(j * peer_slots, peer_slots)
        return pltpu.make_async_remote_copy(
            src_ref=out_buf.at[phase, rows],
            dst_ref=in_buf.at[phase, rows],
            send_sem=dom_send_sem.at[phase, j],
            recv_sem=dom_recv_sem.at[phase, j],
            device_id=(d + OFFSETS[j], s),
            device_id_type=MESH,
        )

    def sub_copy(phase, step):
        there = lax.rem(s + step, n_sub)
        source = pl.ds(pl.multiple_of(dom_width + there * sub_slots, 32), sub_slots)
        target = pl.ds(pl.multiple_of(dom_width + s * sub_slots, 32), sub_slots)
        return pltpu.make_async_remote_copy(
            src_ref=out_buf.at[phase, source],
            dst_ref=in_buf.at[phase, target],
            send_sem=sub_send_sem.at[phase, step - 1],
            recv_sem=sub_recv_sem.at[phase, step - 1],
            device_id=(d, there),
            device_id_type=MESH,
        )

    def start_exchange(phase):
        for j in range(PAIRS):

            @pl.when(inside(j))
            def _():
                dom_copy(phase, j).start()

        for step in range(1, n_sub):
            sub_copy(phase, step).start()
        own = pl.ds(pl.multiple_of(dom_width + s * sub_slots, 32), sub_slots)
        in_buf[phase, own, :] = out_buf[phase, own, :]

    def wait_exchange(phase):
        for j in range(PAIRS):
            @pl.when(inside(PAIRS - 1 - j))
            def _():
                dom_copy(phase, j).wait_recv()

            @pl.when(inside(j))
            def _():
                dom_copy(phase, j).wait_send()

            @pl.when(jnp.logical_not(inside(PAIRS - 1 - j)))
            def _():
                in_buf[phase, pl.ds(j * peer_slots, peer_slots), :] = jnp.zeros(
                    (peer_slots, 256), BF
                )

        for step in range(1, n_sub):
            sub_copy(phase, step).wait()

    def flip(rows):
        parts = [
            rows[j * peer_slots : (j + 1) * peer_slots] for j in reversed(range(PAIRS))
        ]
        return jnp.concatenate(parts + [rows[dom_width:]], axis=0)

    def put_forward(phase, values):
        out_buf[phase, :, 0:128] = to_rows(values).astype(BF)

    def to_rows(values):
        padding = jnp.zeros((48, values.shape[1]), F32)
        return jnp.transpose(jnp.concatenate([values, padding], axis=0))

    def put_backward(phase, rows):
        out_buf[phase, :, 128:256] = flip(rows.astype(BF))

    def got_forward(phase):
        return jnp.transpose(in_buf[phase, :, 0:128].astype(F32))[:80].astype(BF)

    def got_backward(phase):
        return flip(in_buf[phase, :, 128:256])

    lane = lax.broadcasted_iota(jnp.int32, (1, dom_width), 1)
    dom_list = dom_ref[...]
    for j in range(PAIRS):
        dead = (lane >= j * peer_slots + count_ref[0, j]) & (lane < (j + 1) * peer_slots)
        dom_list = jnp.where(dead, -1, dom_list)
    send_list = jnp.concatenate([dom_list, sub_ref[...]], axis=1)
    for base in range(0, faces, 256):
        send_hot[pl.ds(base, 256), :] = one_hot_rows(send_list, base, 256)
    partner = partner_ref[...]
    for base in range(faces, faces + slots, 256):
        pick[pl.ds(base, 256), :] = one_hot_rows(partner, base, 256)

    face = hot(iota((480, 320), 1) == face_node(iota((480, 1), 0)))
    face_t = hot(iota((320, 480), 0) == face_node(iota((1, 480), 1)))

    def traces_of(field_b):
        return to_wide(mm(face, field_b), elements).astype(BF)

    def jump_grad_of(g):
        high, low = split(g)
        values = to_wide(mm(face, high) + mm(face, low), elements)
        return mix(flux_ref, lift_gain * values, True)

    pick_near = pick.at[pl.ds(0, faces)]
    pick_far = pick.at[pl.ds(faces, slots)]

    field0 = w_ref[...].astype(BF)
    traces0 = traces_of(field0)
    put_forward(0, mm(traces0, send_hot[...]))
    jump0 = jump_grad_of(ct_ref[...])
    jump0_s[...] = jump0
    jump0_rows = to_rows(jump0).astype(BF)
    put_backward(0, mm(pick_far[...], jump0_rows))
    pl.semaphore_wait(barrier, expected)
    start_exchange(0)

    for base in range(0, faces, 256):
        pick[pl.ds(base, 256), :] = one_hot_rows(partner, base, 256)
    near[...] = mm(traces0, pick_near[...]) - traces0.astype(F32)
    grad_near[...] = mm(pick_near[...], jump0_rows)

    e1 = hot((iota((1024, 64), 0) & 63) == iota((1024, 64), 1))
    e1t = hot((iota((64, 1024), 1) & 63) == iota((64, 1024), 0))
    e2 = hot((iota((10, 160), 1) >> 4) == iota((10, 160), 0))
    e2t = hot((iota((160, 10), 0) >> 4) == iota((160, 10), 1))
    e3 = hot((iota((5, 80), 1) >> 4) == iota((5, 80), 0))
    e3t = hot((iota((80, 5), 0) >> 4) == iota((80, 5), 1))
    in_wt, mid_w, out_w = in_wt_ref[...], mid_w_ref[...], out_w_ref[...]

    def masked(values, mask):
        return jnp.where(mask, values, 0.0).astype(BF)

    w1[...] = masked(
        mm(mm_nt(e1, in_wt).astype(BF), e2),
        (iota((1024, 160), 0) >> 6) == (iota((1024, 160), 1) & 15),
    )
    w1t[...] = masked(
        mm(mm(e2t, in_wt).astype(BF), e1t),
        (iota((160, 1024), 1) >> 6) == (iota((160, 1024), 0) & 15),
    )
    o16[...] = masked(
        mm(mm(e3t, out_w).astype(BF), e1t),
        (iota((80, 1024), 1) >> 6) == (iota((80, 1024), 0) & 15),
    )
    o16t[...] = masked(
        mm(mm_nt(e1, out_w).astype(BF), e3),
        (iota((1024, 80), 0) >> 6) == (iota((1024, 80), 1) & 15),
    )
    same = (iota((256, 256), 0) >> 6) == (iota((256, 256), 1) >> 6)
    m4[...] = masked(mm(mm(e1[:256], mid_w).astype(BF), e1t[:, :256]), same)
    m4t[...] = masked(mm(mm_nt(e1[:256], mid_w).astype(BF), e1t[:, :256]), same)
    diag = (iota((256, 64), 0) & 63) == iota((256, 64), 1)
    for bias_ref, target in ((in_b_ref, bias1), (mid_b_ref, bias2)):
        column = jnp.sum(jnp.where(diag, bias_ref[...], 0.0), axis=1, keepdims=True)
        target[...] = jnp.broadcast_to(column, target.shape)

    def activations(x, sub):
        h1 = jnp.tanh(mm(w1[pl.ds(sub * 256, 256), :], x) + bias1[...])
        h2 = jnp.tanh(mm(m4[...], h1.astype(BF)) + bias2[...])
        return h1, h2

    def back(upstream, sub, factor1, factor2):
        d2 = (mm(o16t[pl.ds(sub * 256, 256), :], upstream) * factor2).astype(BF)
        d1 = (mm(m4t[...], d2) * factor1).astype(BF)
        return mm(w1t[:, pl.ds(sub * 256, 256)], d1)

    def nodes_of(g):
        return pl.ds(pl.multiple_of(g * 16, 16), 16)

    def set_inputs(field_b, volume_b):
        x_in[0:5] = field_b.reshape(5, 64, elements)
        x_in[5:10] = volume_b.reshape(5, 64, elements)

    volume0 = mm(vol_op_ref[...], field0)
    set_inputs(field0, volume0.astype(BF))

    def forward_group(g, carry):
        x = x_in[:, nodes_of(g), :].reshape(160, elements)
        total = jnp.zeros((80, elements), F32)
        for sub in range(4):
            h1, h2 = activations(x, sub)
            rows = pl.ds(pl.multiple_of(g * 1024 + sub * 256, 256), 256)
            slope1[rows, :] = (1.0 - h1 * h1).astype(BF)
            slope2[rows, :] = (1.0 - h2 * h2).astype(BF)
            total = total + mm(o16[:, pl.ds(sub * 256, 256)], h2.astype(BF))
        clo[:, nodes_of(g), :] = total.reshape(5, 16, elements)
        return carry

    lax.fori_loop(0, 4, forward_group, 0)
    base0 = w_ref[...] + time_step * (volume0 + clo[...].reshape(320, elements))

    wait_exchange(0)
    jump = near[...] + mm(got_forward(0), pick_far[...])
    flux = mix(flux_ref, lift_gain * jump, False)
    middle = base0 + time_step * lift(face_t, flux, elements)
    middle_s[...] = middle
    rows = grad_near[...] + mm(send_hot[...], got_backward(0))
    trace_grad = jnp.transpose(rows)[:80] - jump0_s[...]
    adj_lift = lift(face_t, trace_grad, elements)

    field1 = middle.astype(BF)
    traces1 = traces_of(field1)
    traces_s[...] = traces1
    put_forward(1, mm(traces1, send_hot[...]))
    volume1 = mm(vol_op_ref[...], field1)
    set_inputs(field1, volume1.astype(BF))
    g_in[...] = ct_ref[...].astype(BF).reshape(5, 64, elements)

    def both_group(g, carry):
        x = x_in[:, nodes_of(g), :].reshape(160, elements)
        upstream = g_in[:, nodes_of(g), :].reshape(80, elements)
        total = jnp.zeros((80, elements), F32)
        grads = jnp.zeros((160, elements), F32)
        for sub in range(4):
            h1, h2 = activations(x, sub)
            total = total + mm(o16[:, pl.ds(sub * 256, 256)], h2.astype(BF))
            grads = grads + back(upstream, sub, 1.0 - h1 * h1, 1.0 - h2 * h2)
        clo[:, nodes_of(g), :] = total.reshape(5, 16, elements)
        x_grad[:, nodes_of(g), :] = grads.reshape(10, 16, elements)
        return carry

    lax.fori_loop(0, 4, both_group, 0)

    def input_part(adjoint):
        field_grad = x_grad[0:5].reshape(320, elements)
        volume_grad = x_grad[5:10].reshape(320, elements)
        return mm_tn(vol_op_ref[...], (adjoint + volume_grad).astype(BF)) + field_grad

    ct = ct_ref[...]
    adj_mid = 0.5 * ct + 0.5 * time_step * (input_part(ct) + adj_lift)
    adj_mid_s[...] = adj_mid
    jump1 = jump_grad_of(adj_mid)
    jump1_s[...] = jump1
    jump1_rows = to_rows(jump1).astype(BF)
    put_backward(1, mm(pick_far[...], jump1_rows))
    start_exchange(1)

    final_ref[...] = 0.5 * w_ref[...] + 0.5 * (
        middle_s[...] + time_step * (volume1 + clo[...].reshape(320, elements))
    )
    near[...] = mm(traces_s[...], pick_near[...]) - traces_s[...].astype(F32)
    grad_near[...] = mm(pick_near[...], jump1_rows)
    g_in[...] = adj_mid.astype(BF).reshape(5, 64, elements)

    def back_group(g, carry):
        upstream = g_in[:, nodes_of(g), :].reshape(80, elements)
        grads = jnp.zeros((160, elements), F32)
        for sub in range(4):
            rows = pl.ds(pl.multiple_of(g * 1024 + sub * 256, 256), 256)
            grads = grads + back(
                upstream, sub, slope1[rows, :].astype(F32), slope2[rows, :].astype(F32)
            )
        x_grad[:, nodes_of(g), :] = grads.reshape(10, 16, elements)
        return carry

    lax.fori_loop(0, 4, back_group, 0)
    adj_mid = adj_mid_s[...]
    adj_ref[...] = 0.5 * ct_ref[...] + adj_mid + time_step * input_part(adj_mid)

    wait_exchange(1)
    jump = near[...] + mm(got_forward(1), pick_far[...])
    flux = mix(flux_ref, lift_gain * jump, False)
    final_ref[...] += 0.5 * time_step * lift(face_t, flux, elements)
    rows = grad_near[...] + mm(send_hot[...], got_backward(1))
    trace_grad = jnp.transpose(rows)[:80] - jump1_s[...]
    adj_ref[...] += time_step * lift(face_t, trace_grad, elements)


def body(
    n_dom,
    n_sub,
    initial_state,
    cotangent,
    volume_operator,
    in_weight,
    in_bias,
    mid_weight,
    mid_bias,
    out_weight,
    flux_matrix,
    dom_send,
    dom_count,
    sub_send,
    partner,
):
    elements = initial_state.shape[1]
    faces = 6 * elements
    slots = dom_send.shape[1] + sub_send.shape[1]
    vmem = pl.BlockSpec(memory_space=pltpu.VMEM)
    smem = pl.BlockSpec(memory_space=pltpu.SMEM)
    state = jax.ShapeDtypeStruct(initial_state.shape, F32)
    return pl.pallas_call(
        functools.partial(kernel, n_dom, n_sub),
        out_shape=(state, state),
        in_specs=[vmem] * 8 + [smem, vmem, smem] + [vmem] * 2,
        out_specs=(vmem, vmem),
        scratch_shapes=[
            pltpu.VMEM((faces + slots, faces), BF),
            pltpu.VMEM((faces, slots), BF),
            pltpu.VMEM((1024, 160), BF),
            pltpu.VMEM((160, 1024), BF),
            pltpu.VMEM((256, 256), BF),
            pltpu.VMEM((256, 256), BF),
            pltpu.VMEM((80, 1024), BF),
            pltpu.VMEM((1024, 80), BF),
            pltpu.VMEM((256, elements), F32),
            pltpu.VMEM((256, elements), F32),
            pltpu.VMEM((10, 64, elements), BF),
            pltpu.VMEM((5, 64, elements), BF),
            pltpu.VMEM((5, 64, elements), F32),
            pltpu.VMEM((10, 64, elements), F32),
            pltpu.VMEM((4096, elements), BF),
            pltpu.VMEM((4096, elements), BF),
            pltpu.VMEM((80, faces), BF),
            pltpu.VMEM((80, faces), F32),
            pltpu.VMEM((faces, 128), F32),
            pltpu.VMEM((80, faces), F32),
            pltpu.VMEM((80, faces), F32),
            pltpu.VMEM(initial_state.shape, F32),
            pltpu.VMEM(initial_state.shape, F32),
            pltpu.VMEM((2, slots, 256), BF),
            pltpu.VMEM((2, slots, 256), BF),
            pltpu.SemaphoreType.DMA((2, PAIRS)),
            pltpu.SemaphoreType.DMA((2, PAIRS)),
            pltpu.SemaphoreType.DMA((2, n_sub - 1)),
            pltpu.SemaphoreType.DMA((2, n_sub - 1)),
        ],
        compiler_params=pltpu.CompilerParams(
            collective_id=0, has_side_effects=True, vmem_limit_bytes=32 * 1024 * 1024
        ),
        cost_estimate=pl.CostEstimate(
            flops=8_000_000_000, bytes_accessed=4_000_000, transcendentals=4_000_000
        ),
    )(
        initial_state,
        cotangent,
        volume_operator,
        in_weight.T,
        in_bias.reshape(1, -1),
        mid_weight,
        mid_bias.reshape(1, -1),
        out_weight,
        flux_matrix,
        dom_send,
        dom_count,
        sub_send,
        partner,
    )


def solution(mesh):
    return jax.shard_map(
        functools.partial(body, mesh.shape["dom"], mesh.shape["sub"]),
        mesh=mesh,
        in_specs=(
            P(None, ("dom", "sub")),
            P(None, ("dom", "sub")),
            P(),
            P(),
            P(),
            P(),
            P(),
            P(),
            P(),
            P("dom", "sub"),
            P("dom", "sub"),
            P("dom", "sub"),
            P("dom", "sub"),
        ),
        out_specs=(P(None, ("dom", "sub")), P(None, ("dom", "sub"))),
        check_vma=False,
    )
```

```python
import functools

import jax
import jax.numpy as jnp
from jax import lax
from jax.experimental import pallas as pl
from jax.experimental.pallas import tpu as pltpu
from jax.sharding import PartitionSpec as P

REACH = 4
OFFSETS = [offset for offset in range(-REACH, REACH + 1) if offset != 0]
PAIRS = len(OFFSETS)
MESH = pl.DeviceIdType.MESH

time_step = 0.4
lift_gain = 1.5
BF = jnp.bfloat16
F32 = jnp.float32


def iota(shape, axis):
    return lax.broadcasted_iota(jnp.int32, shape, axis)


def hot(mask):
    return jnp.where(mask, 1.0, 0.0).astype(BF)


def face_node(row):
    f = sum((row >= 80 * i).astype(jnp.int32) for i in range(1, 6))
    within = row - 80 * f
    v, k = within >> 4, within & 15
    end = f & 1
    node = jnp.where(
        f < 2,
        3 * end + 4 * k,
        jnp.where(f < 4, (k & 3) + 16 * (k >> 2) + 12 * end, k + 48 * end),
    )
    return 64 * v + node


def mm(a, b):
    return jnp.dot(a, b, preferred_element_type=F32)


def mm_nt(a, b):
    return lax.dot_general(a, b, (((1,), (1,)), ((), ())), preferred_element_type=F32)


def mm_tn(a, b):
    return lax.dot_general(a, b, (((0,), (0,)), ((), ())), preferred_element_type=F32)


def split(values):
    high = values.astype(BF)
    return high, (values - high.astype(F32)).astype(BF)


def to_wide(faces, elements):
    return jnp.concatenate([faces[f * 80 : (f + 1) * 80] for f in range(6)], axis=1)


def to_tall(wide, elements):
    return jnp.concatenate(
        [wide[:, f * elements : (f + 1) * elements] for f in range(6)], axis=0
    )


def lift(face_t, wide, elements):
    high, low = split(to_tall(wide, elements))
    return mm(face_t, high) + mm(face_t, low)


def mix(flux_ref, values, transposed):
    rows = []
    for v in range(5):
        total = None
        for u in range(5):
            weight = flux_ref[u, v] if transposed else flux_ref[v, u]
            term = weight * values[u * 16 : (u + 1) * 16]
            total = term if total is None else total + term
        rows.append(total)
    return jnp.concatenate(rows, axis=0)


def one_hot_rows(row_list, base, rows):
    width = row_list.shape[1]
    shifted = (row_list - base).astype(F32)
    wide = jnp.broadcast_to(shifted, (rows, width))
    spot = lax.broadcasted_iota(jnp.int32, (rows, width), 0).astype(F32)
    return jnp.where(wide == spot, 1.0, 0.0).astype(BF)


def kernel(
    n_dom,
    n_sub,
    w_ref,
    ct_ref,
    vol_op_ref,
    in_wt_ref,
    in_b_ref,
    mid_w_ref,
    mid_b_ref,
    out_w_ref,
    flux_ref,
    dom_ref,
    count_ref,
    sub_ref,
    partner_ref,
    final_ref,
    adj_ref,
    pick,
    send_hot,
    w1,
    w1t,
    m4,
    m4t,
    o16,
    o16t,
    x_in,
    g_in,
    clo,
    x_grad,
    slope1,
    slope2,
    traces_s,
    near,
    grad_near,
    jump0_s,
    jump1_s,
    middle_s,
    adj_mid_s,
    out_buf,
    in_buf,
    dom_send_sem,
    dom_recv_sem,
    sub_send_sem,
    sub_recv_sem,
):
    elements = w_ref.shape[1]
    faces = 6 * elements
    dom_width = dom_ref.shape[1]
    peer_slots = dom_width // PAIRS
    sub_width = sub_ref.shape[1]
    sub_slots = sub_width // n_sub
    slots = dom_width + sub_width
    d = lax.axis_index("dom")
    s = lax.axis_index("sub")

    def inside(j):
        target = d + OFFSETS[j]
        return (target >= 0) & (target < n_dom)

    barrier = pltpu.get_barrier_semaphore()
    expected = n_sub - 1
    for j in range(PAIRS):
        expected = expected + jnp.where(inside(j), 1, 0)

        @pl.when(inside(j))
        def _():
            pl.semaphore_signal(
                barrier, inc=1, device_id=(d + OFFSETS[j], s), device_id_type=MESH
            )

    for step in range(1, n_sub):
        pl.semaphore_signal(
            barrier, inc=1, device_id=(d, lax.rem(s + step, n_sub)), device_id_type=MESH
        )

    def dom_copy(phase, j):
        rows = pl.ds(j * peer_slots, peer_slots)
        return pltpu.make_async_remote_copy(
            src_ref=out_buf.at[phase, rows],
            dst_ref=in_buf.at[phase, rows],
            send_sem=dom_send_sem.at[phase, j],
            recv_sem=dom_recv_sem.at[phase, j],
            device_id=(d + OFFSETS[j], s),
            device_id_type=MESH,
        )

    def sub_copy(phase, step):
        there = lax.rem(s + step, n_sub)
        source = pl.ds(pl.multiple_of(dom_width + there * sub_slots, 32), sub_slots)
        target = pl.ds(pl.multiple_of(dom_width + s * sub_slots, 32), sub_slots)
        return pltpu.make_async_remote_copy(
            src_ref=out_buf.at[phase, source],
            dst_ref=in_buf.at[phase, target],
            send_sem=sub_send_sem.at[phase, step - 1],
            recv_sem=sub_recv_sem.at[phase, step - 1],
            device_id=(d, there),
            device_id_type=MESH,
        )

    def start_exchange(phase):
        for j in range(PAIRS):

            @pl.when(inside(j))
            def _():
                dom_copy(phase, j).start()

        for step in range(1, n_sub):
            sub_copy(phase, step).start()
        own = pl.ds(pl.multiple_of(dom_width + s * sub_slots, 32), sub_slots)
        in_buf[phase, own, :] = out_buf[phase, own, :]

    def wait_exchange(phase):
        for j in range(PAIRS):
            @pl.when(inside(PAIRS - 1 - j))
            def _():
                dom_copy(phase, j).wait_recv()

            @pl.when(inside(j))
            def _():
                dom_copy(phase, j).wait_send()

            @pl.when(jnp.logical_not(inside(PAIRS - 1 - j)))
            def _():
                in_buf[phase, pl.ds(j * peer_slots, peer_slots), :] = jnp.zeros(
                    (peer_slots, 256), BF
                )

        for step in range(1, n_sub):
            sub_copy(phase, step).wait()

    def flip(rows):
        parts = [
            rows[j * peer_slots : (j + 1) * peer_slots] for j in reversed(range(PAIRS))
        ]
        return jnp.concatenate(parts + [rows[dom_width:]], axis=0)

    def put_forward(phase, values):
        out_buf[phase, :, 0:128] = to_rows(values).astype(BF)

    def to_rows(values):
        padding = jnp.zeros((48, values.shape[1]), F32)
        return jnp.transpose(jnp.concatenate([values, padding], axis=0))

    def put_backward(phase, rows):
        out_buf[phase, :, 128:256] = flip(rows.astype(BF))

    def got_forward(phase):
        return jnp.transpose(in_buf[phase, :, 0:128].astype(F32))[:80].astype(BF)

    def got_backward(phase):
        return flip(in_buf[phase, :, 128:256])

    lane = lax.broadcasted_iota(jnp.int32, (1, dom_width), 1)
    dom_list = dom_ref[...]
    for j in range(PAIRS):
        dead = (lane >= j * peer_slots + count_ref[0, j]) & (lane < (j + 1) * peer_slots)
        dom_list = jnp.where(dead, -1, dom_list)
    send_list = jnp.concatenate([dom_list, sub_ref[...]], axis=1)
    for base in range(0, faces, 256):
        send_hot[pl.ds(base, 256), :] = one_hot_rows(send_list, base, 256)
    partner = partner_ref[...]
    for base in range(faces, faces + slots, 256):
        pick[pl.ds(base, 256), :] = one_hot_rows(partner, base, 256)

    face = hot(iota((480, 320), 1) == face_node(iota((480, 1), 0)))
    face_t = hot(iota((320, 480), 0) == face_node(iota((1, 480), 1)))

    def traces_of(field_b):
        return to_wide(mm(face, field_b), elements).astype(BF)

    def jump_grad_of(g):
        high, low = split(g)
        values = to_wide(mm(face, high) + mm(face, low), elements)
        return mix(flux_ref, lift_gain * values, True)

    pick_near = pick.at[pl.ds(0, faces)]
    pick_far = pick.at[pl.ds(faces, slots)]

    field0 = w_ref[...].astype(BF)
    traces0 = traces_of(field0)
    put_forward(0, mm(traces0, send_hot[...]))
    jump0 = jump_grad_of(ct_ref[...])
    jump0_s[...] = jump0
    jump0_rows = to_rows(jump0).astype(BF)
    put_backward(0, mm(pick_far[...], jump0_rows))
    pl.semaphore_wait(barrier, expected)
    start_exchange(0)

    for base in range(0, faces, 256):
        pick[pl.ds(base, 256), :] = one_hot_rows(partner, base, 256)
    near[...] = mm(traces0, pick_near[...]) - traces0.astype(F32)
    grad_near[...] = mm(pick_near[...], jump0_rows)

    e1 = hot((iota((1024, 64), 0) & 63) == iota((1024, 64), 1))
    e1t = hot((iota((64, 1024), 1) & 63) == iota((64, 1024), 0))
    e2 = hot((iota((10, 256), 1) >> 4) == iota((10, 256), 0))
    e2t = hot((iota((256, 10), 0) >> 4) == iota((256, 10), 1))
    e3 = hot((iota((5, 128), 1) >> 4) == iota((5, 128), 0))
    e3t = hot((iota((128, 5), 0) >> 4) == iota((128, 5), 1))
    in_wt, mid_w, out_w = in_wt_ref[...], mid_w_ref[...], out_w_ref[...]

    def masked(values, mask):
        return jnp.where(mask, values, 0.0).astype(BF)

    def node_match(shape, hidden_axis):
        hidden = iota(shape, hidden_axis) >> 6
        return hidden == (iota(shape, 1 - hidden_axis) & 15)

    w1[...] = masked(mm(mm_nt(e1, in_wt).astype(BF), e2), node_match((1024, 256), 0))
    w1t[...] = masked(mm(mm(e2t, in_wt).astype(BF), e1t), node_match((256, 1024), 1))
    o16[...] = masked(mm(mm(e3t, out_w).astype(BF), e1t), node_match((128, 1024), 1))
    o16t[...] = masked(mm(mm_nt(e1, out_w).astype(BF), e3), node_match((1024, 128), 0))
    same = (iota((256, 256), 0) >> 6) == (iota((256, 256), 1) >> 6)
    m4[...] = masked(mm(mm(e1[:256], mid_w).astype(BF), e1t[:, :256]), same)
    m4t[...] = masked(mm(mm_nt(e1[:256], mid_w).astype(BF), e1t[:, :256]), same)
    bias1 = jnp.concatenate([in_b_ref[...]] * 4, axis=1)
    bias2 = jnp.concatenate([mid_b_ref[...]] * 4, axis=1)

    def group_rows(parts, width):
        blocks = []
        for g in range(4):
            picked = [
                part.reshape(5, 64, elements)[:, 16 * g : 16 * g + 16].reshape(80, elements)
                for part in parts
            ]
            padding = jnp.zeros((width - 80 * len(parts), elements), F32)
            blocks.append(jnp.transpose(jnp.concatenate(picked + [padding], axis=0)))
        return jnp.concatenate(blocks, axis=0).astype(BF)

    def ungroup(rows_ref, part):
        blocks = []
        for g in range(4):
            block = jnp.transpose(rows_ref[pl.ds(g * elements, elements), :])
            blocks.append(block[80 * part : 80 * part + 80].reshape(5, 16, elements))
        return jnp.concatenate(blocks, axis=1).reshape(320, elements)

    def columns_of(sub):
        return pl.ds(pl.multiple_of(sub * 256, 256), 256)

    def activations(sub):
        h1 = jnp.tanh(mm(x_in[...], w1t[:, columns_of(sub)]) + bias1)
        h2 = jnp.tanh(mm(h1.astype(BF), m4t[...]) + bias2)
        return h1, h2

    def back(sub, factor1, factor2):
        d2 = (mm(g_in[...], o16[:, columns_of(sub)]) * factor2).astype(BF)
        d1 = (mm(d2, m4[...]) * factor1).astype(BF)
        x_grad[...] += mm(d1, w1[columns_of(sub), :])

    volume0 = mm(vol_op_ref[...], field0)
    x_in[...] = group_rows([field0.astype(F32), volume0], 256)
    clo[...] = jnp.zeros_like(clo)

    def forward_step(sub, carry):
        h1, h2 = activations(sub)
        slope1[sub] = (1.0 - h1 * h1).astype(BF)
        slope2[sub] = (1.0 - h2 * h2).astype(BF)
        clo[...] += mm(h2.astype(BF), o16t[columns_of(sub), :])
        return carry

    lax.fori_loop(0, 4, forward_step, 0)
    base0 = w_ref[...] + time_step * (volume0 + ungroup(clo, 0))

    wait_exchange(0)
    jump = near[...] + mm(got_forward(0), pick_far[...])
    flux = mix(flux_ref, lift_gain * jump, False)
    middle = base0 + time_step * lift(face_t, flux, elements)
    middle_s[...] = middle
    rows = grad_near[...] + mm(send_hot[...], got_backward(0))
    trace_grad = jnp.transpose(rows)[:80] - jump0_s[...]
    adj_lift = lift(face_t, trace_grad, elements)

    field1 = middle.astype(BF)
    traces1 = traces_of(field1)
    traces_s[...] = traces1
    put_forward(1, mm(traces1, send_hot[...]))
    volume1 = mm(vol_op_ref[...], field1)
    x_in[...] = group_rows([field1.astype(F32), volume1], 256)
    g_in[...] = group_rows([ct_ref[...]], 128)
    clo[...] = jnp.zeros_like(clo)
    x_grad[...] = jnp.zeros_like(x_grad)

    def both_step(sub, carry):
        h1, h2 = activations(sub)
        clo[...] += mm(h2.astype(BF), o16t[columns_of(sub), :])
        back(sub, 1.0 - h1 * h1, 1.0 - h2 * h2)
        return carry

    lax.fori_loop(0, 4, both_step, 0)

    def input_part(adjoint):
        field_grad, volume_grad = ungroup(x_grad, 0), ungroup(x_grad, 1)
        return mm_tn(vol_op_ref[...], (adjoint + volume_grad).astype(BF)) + field_grad

    ct = ct_ref[...]
    adj_mid = 0.5 * ct + 0.5 * time_step * (input_part(ct) + adj_lift)
    adj_mid_s[...] = adj_mid
    jump1 = jump_grad_of(adj_mid)
    jump1_s[...] = jump1
    jump1_rows = to_rows(jump1).astype(BF)
    put_backward(1, mm(pick_far[...], jump1_rows))
    start_exchange(1)

    final_ref[...] = 0.5 * w_ref[...] + 0.5 * (
        middle_s[...] + time_step * (volume1 + ungroup(clo, 0))
    )
    near[...] = mm(traces_s[...], pick_near[...]) - traces_s[...].astype(F32)
    grad_near[...] = mm(pick_near[...], jump1_rows)
    g_in[...] = group_rows([adj_mid], 128)
    x_grad[...] = jnp.zeros_like(x_grad)

    def back_step(sub, carry):
        back(sub, slope1[sub].astype(F32), slope2[sub].astype(F32))
        return carry

    lax.fori_loop(0, 4, back_step, 0)
    adj_mid = adj_mid_s[...]
    adj_ref[...] = 0.5 * ct_ref[...] + adj_mid + time_step * input_part(adj_mid)

    wait_exchange(1)
    jump = near[...] + mm(got_forward(1), pick_far[...])
    flux = mix(flux_ref, lift_gain * jump, False)
    final_ref[...] += 0.5 * time_step * lift(face_t, flux, elements)
    rows = grad_near[...] + mm(send_hot[...], got_backward(1))
    trace_grad = jnp.transpose(rows)[:80] - jump1_s[...]
    adj_ref[...] += time_step * lift(face_t, trace_grad, elements)


def body(
    n_dom,
    n_sub,
    initial_state,
    cotangent,
    volume_operator,
    in_weight,
    in_bias,
    mid_weight,
    mid_bias,
    out_weight,
    flux_matrix,
    dom_send,
    dom_count,
    sub_send,
    partner,
):
    elements = initial_state.shape[1]
    faces = 6 * elements
    slots = dom_send.shape[1] + sub_send.shape[1]
    vmem = pl.BlockSpec(memory_space=pltpu.VMEM)
    smem = pl.BlockSpec(memory_space=pltpu.SMEM)
    state = jax.ShapeDtypeStruct(initial_state.shape, F32)
    return pl.pallas_call(
        functools.partial(kernel, n_dom, n_sub),
        out_shape=(state, state),
        in_specs=[vmem] * 8 + [smem, vmem, smem] + [vmem] * 2,
        out_specs=(vmem, vmem),
        scratch_shapes=[
            pltpu.VMEM((faces + slots, faces), BF),
            pltpu.VMEM((faces, slots), BF),
            pltpu.VMEM((1024, 256), BF),
            pltpu.VMEM((256, 1024), BF),
            pltpu.VMEM((256, 256), BF),
            pltpu.VMEM((256, 256), BF),
            pltpu.VMEM((128, 1024), BF),
            pltpu.VMEM((1024, 128), BF),
            pltpu.VMEM((4 * elements, 256), BF),
            pltpu.VMEM((4 * elements, 128), BF),
            pltpu.VMEM((4 * elements, 128), F32),
            pltpu.VMEM((4 * elements, 256), F32),
            pltpu.VMEM((4, 4 * elements, 256), BF),
            pltpu.VMEM((4, 4 * elements, 256), BF),
            pltpu.VMEM((80, faces), BF),
            pltpu.VMEM((80, faces), F32),
            pltpu.VMEM((faces, 128), F32),
            pltpu.VMEM((80, faces), F32),
            pltpu.VMEM((80, faces), F32),
            pltpu.VMEM(initial_state.shape, F32),
            pltpu.VMEM(initial_state.shape, F32),
            pltpu.VMEM((2, slots, 256), BF),
            pltpu.VMEM((2, slots, 256), BF),
            pltpu.SemaphoreType.DMA((2, PAIRS)),
            pltpu.SemaphoreType.DMA((2, PAIRS)),
            pltpu.SemaphoreType.DMA((2, n_sub - 1)),
            pltpu.SemaphoreType.DMA((2, n_sub - 1)),
        ],
        compiler_params=pltpu.CompilerParams(
            collective_id=0, has_side_effects=True, vmem_limit_bytes=56 * 1024 * 1024
        ),
        cost_estimate=pl.CostEstimate(
            flops=8_000_000_000, bytes_accessed=4_000_000, transcendentals=4_000_000
        ),
    )(
        initial_state,
        cotangent,
        volume_operator,
        in_weight.T,
        in_bias.reshape(1, -1),
        mid_weight,
        mid_bias.reshape(1, -1),
        out_weight,
        flux_matrix,
        dom_send,
        dom_count,
        sub_send,
        partner,
    )


def solution(mesh):
    return jax.shard_map(
        functools.partial(body, mesh.shape["dom"], mesh.shape["sub"]),
        mesh=mesh,
        in_specs=(
            P(None, ("dom", "sub")),
            P(None, ("dom", "sub")),
            P(),
            P(),
            P(),
            P(),
            P(),
            P(),
            P(),
            P("dom", "sub"),
            P("dom", "sub"),
            P("dom", "sub"),
            P("dom", "sub"),
        ),
        out_specs=(P(None, ("dom", "sub")), P(None, ("dom", "sub"))),
        check_vma=False,
    )
```

```python
import functools

import jax
import jax.numpy as jnp
from jax import lax
from jax.experimental import pallas as pl
from jax.experimental.pallas import tpu as pltpu
from jax.sharding import PartitionSpec as P

REACH = 4
OFFSETS = [offset for offset in range(-REACH, REACH + 1) if offset != 0]
PAIRS = len(OFFSETS)
MESH = pl.DeviceIdType.MESH

time_step = 0.4
lift_gain = 1.5
BF = jnp.bfloat16
F32 = jnp.float32


def iota(shape, axis):
    return lax.broadcasted_iota(jnp.int32, shape, axis)


def hot(mask):
    return jnp.where(mask, 1.0, 0.0).astype(BF)


def face_node(row):
    f = sum((row >= 80 * i).astype(jnp.int32) for i in range(1, 6))
    within = row - 80 * f
    v, k = within >> 4, within & 15
    end = f & 1
    node = jnp.where(
        f < 2,
        3 * end + 4 * k,
        jnp.where(f < 4, (k & 3) + 16 * (k >> 2) + 12 * end, k + 48 * end),
    )
    return 64 * v + node


def mm(a, b):
    return jnp.dot(a, b, preferred_element_type=F32)


def mm_nt(a, b):
    return lax.dot_general(a, b, (((1,), (1,)), ((), ())), preferred_element_type=F32)


def mm_tn(a, b):
    return lax.dot_general(a, b, (((0,), (0,)), ((), ())), preferred_element_type=F32)


def split(values):
    high = values.astype(BF)
    return high, (values - high.astype(F32)).astype(BF)


def to_wide(faces, elements):
    return jnp.concatenate([faces[f * 80 : (f + 1) * 80] for f in range(6)], axis=1)


def to_tall(wide, elements):
    return jnp.concatenate(
        [wide[:, f * elements : (f + 1) * elements] for f in range(6)], axis=0
    )


def lift(face_t, tall):
    high, low = split(tall)
    return mm(face_t, high) + mm(face_t, low)


def mix(flux_ref, values, transposed):
    rows = []
    for v in range(5):
        total = None
        for u in range(5):
            weight = flux_ref[u, v] if transposed else flux_ref[v, u]
            term = weight * values[u * 16 : (u + 1) * 16]
            total = term if total is None else total + term
        rows.append(total)
    return jnp.concatenate(rows, axis=0)


def one_hot_lanes(row_list):
    width = row_list.shape[1]
    low = jnp.broadcast_to(row_list & 255, (256, width))
    return jnp.where(low == iota((256, width), 0), 1.0, 0.0)


def pick_columns(blocks, low_hot, high, first):
    picked = []
    for base in range(0, high.shape[1], 256):
        products = mm(blocks, low_hot[:, base : base + 256])
        mine = high[:, base : base + 256]
        total = jnp.zeros((80, 256), F32)
        for b in range(blocks.shape[0] // 80):
            total = jnp.where(mine == first + b, products[b * 80 : (b + 1) * 80], total)
        picked.append(total)
    return jnp.concatenate(picked, axis=1)


def add_columns(values, low_hot_t, high, first, count):
    parts = [
        values * jnp.where(high == first + b, 1.0, 0.0).astype(BF) for b in range(count)
    ]
    return mm(jnp.concatenate(parts, axis=0), low_hot_t[...])


def kernel(
    n_dom,
    n_sub,
    w_ref,
    ct_ref,
    vol_op_ref,
    in_wt_ref,
    in_b_ref,
    mid_w_ref,
    mid_b_ref,
    out_w_ref,
    flux_ref,
    dom_ref,
    count_ref,
    sub_ref,
    partner_ref,
    final_ref,
    adj_ref,
    link_hot,
    link_hot_t,
    send_hot,
    send_hot_t,
    w1,
    w1t,
    m4,
    m4t,
    o16,
    o16t,
    x_in,
    g_in,
    clo,
    x_grad,
    slope1,
    slope2,
    traces_s,
    near,
    grad_near,
    middle_s,
    adj_mid_s,
    out_buf,
    in_buf,
    dom_send_sem,
    dom_recv_sem,
    sub_send_sem,
    sub_recv_sem,
):
    elements = w_ref.shape[1]
    faces = 6 * elements
    dom_width = dom_ref.shape[1]
    peer_slots = dom_width // PAIRS
    sub_width = sub_ref.shape[1]
    sub_slots = sub_width // n_sub
    slots = dom_width + sub_width
    d = lax.axis_index("dom")
    s = lax.axis_index("sub")

    def inside(j):
        target = d + OFFSETS[j]
        return (target >= 0) & (target < n_dom)

    barrier = pltpu.get_barrier_semaphore()
    expected = n_sub - 1
    for j in range(PAIRS):
        expected = expected + jnp.where(inside(j), 1, 0)

        @pl.when(inside(j))
        def _():
            pl.semaphore_signal(
                barrier, inc=1, device_id=(d + OFFSETS[j], s), device_id_type=MESH
            )

    for step in range(1, n_sub):
        pl.semaphore_signal(
            barrier, inc=1, device_id=(d, lax.rem(s + step, n_sub)), device_id_type=MESH
        )

    def dom_copy(phase, j):
        rows = pl.ds(j * peer_slots, peer_slots)
        return pltpu.make_async_remote_copy(
            src_ref=out_buf.at[phase, rows],
            dst_ref=in_buf.at[phase, rows],
            send_sem=dom_send_sem.at[phase, j],
            recv_sem=dom_recv_sem.at[phase, j],
            device_id=(d + OFFSETS[j], s),
            device_id_type=MESH,
        )

    def sub_copy(phase, step):
        there = lax.rem(s + step, n_sub)
        source = pl.ds(pl.multiple_of(dom_width + there * sub_slots, 32), sub_slots)
        target = pl.ds(pl.multiple_of(dom_width + s * sub_slots, 32), sub_slots)
        return pltpu.make_async_remote_copy(
            src_ref=out_buf.at[phase, source],
            dst_ref=in_buf.at[phase, target],
            send_sem=sub_send_sem.at[phase, step - 1],
            recv_sem=sub_recv_sem.at[phase, step - 1],
            device_id=(d, there),
            device_id_type=MESH,
        )

    def start_exchange(phase):
        for j in range(PAIRS):

            @pl.when(inside(j))
            def _():
                dom_copy(phase, j).start()

        for step in range(1, n_sub):
            sub_copy(phase, step).start()
        own = pl.ds(pl.multiple_of(dom_width + s * sub_slots, 32), sub_slots)
        in_buf[phase, own, :] = out_buf[phase, own, :]

    def wait_exchange(phase):
        for j in range(PAIRS):
            @pl.when(inside(PAIRS - 1 - j))
            def _():
                dom_copy(phase, j).wait_recv()

            @pl.when(inside(j))
            def _():
                dom_copy(phase, j).wait_send()

            @pl.when(jnp.logical_not(inside(PAIRS - 1 - j)))
            def _():
                in_buf[phase, pl.ds(j * peer_slots, peer_slots), :] = jnp.zeros(
                    (peer_slots, 256), BF
                )

        for step in range(1, n_sub):
            sub_copy(phase, step).wait()

    def flip(rows):
        parts = [
            rows[j * peer_slots : (j + 1) * peer_slots] for j in reversed(range(PAIRS))
        ]
        return jnp.concatenate(parts + [rows[dom_width:]], axis=0)

    def put_forward(phase, values):
        out_buf[phase, :, 0:128] = to_rows(values).astype(BF)

    def to_rows(values):
        padding = jnp.zeros((48, values.shape[1]), F32)
        return jnp.transpose(jnp.concatenate([values, padding], axis=0))

    def put_backward(phase, blocks):
        wide = jnp.concatenate(
            [blocks[80 * b : 80 * b + 80] for b in range(slots // 256)], axis=1
        )
        out_buf[phase, :, 128:256] = flip(to_rows(wide)).astype(BF)

    def got_forward(phase):
        wide = jnp.transpose(in_buf[phase, :, 0:128].astype(F32))[:80].astype(BF)
        return jnp.concatenate([wide[:, b : b + 256] for b in range(0, slots, 256)], axis=0)

    def got_backward(phase):
        rows = flip(in_buf[phase, :, 128:256].astype(F32))
        return jnp.transpose(rows)[:80].astype(BF)

    lane = lax.broadcasted_iota(jnp.int32, (1, dom_width), 1)
    dom_list = dom_ref[...]
    for j in range(PAIRS):
        dead = (lane >= j * peer_slots + count_ref[0, j]) & (lane < (j + 1) * peer_slots)
        dom_list = jnp.where(dead, -1, dom_list)
    send_list = jnp.concatenate([dom_list, sub_ref[...]], axis=1)
    send_low = one_hot_lanes(send_list)
    send_hot[...] = send_low.astype(BF)
    send_hot_t[...] = jnp.transpose(send_low).astype(BF)
    send_high = send_list >> 8
    partner = partner_ref[...]
    link_low = one_hot_lanes(partner)
    link_hot[...] = link_low.astype(BF)
    link_hot_t[...] = jnp.transpose(link_low).astype(BF)
    link_high = partner >> 8
    far_count = slots // 256

    face = hot(iota((480, 320), 1) == face_node(iota((480, 1), 0)))
    face_t = hot(iota((320, 480), 0) == face_node(iota((1, 480), 1)))

    def traces_of(field_b):
        return mm(face, field_b).astype(BF)

    def jump_grad_of(g):
        high, low = split(g)
        values = to_wide(mm(face, high) + mm(face, low), elements)
        return mix(flux_ref, lift_gain * values, True)

    field0 = w_ref[...].astype(BF)
    traces0 = traces_of(field0)
    put_forward(0, pick_columns(traces0, send_hot, send_high, 0))
    jump0 = jump_grad_of(ct_ref[...])
    jump0_b = jump0.astype(BF)
    put_backward(0, add_columns(jump0_b, link_hot_t, link_high, 6, far_count))
    pl.semaphore_wait(barrier, expected)
    start_exchange(0)

    near[...] = pick_columns(traces0, link_hot, link_high, 0) - to_wide(
        traces0.astype(F32), elements
    )
    grad_near[...] = add_columns(jump0_b, link_hot_t, link_high, 0, 6) - to_tall(
        jump0, elements
    )

    e1 = hot((iota((1024, 64), 0) & 63) == iota((1024, 64), 1))
    e1t = hot((iota((64, 1024), 1) & 63) == iota((64, 1024), 0))
    e2 = hot((iota((10, 256), 1) >> 4) == iota((10, 256), 0))
    e2t = hot((iota((256, 10), 0) >> 4) == iota((256, 10), 1))
    e3 = hot((iota((5, 128), 1) >> 4) == iota((5, 128), 0))
    e3t = hot((iota((128, 5), 0) >> 4) == iota((128, 5), 1))
    in_wt, mid_w, out_w = in_wt_ref[...], mid_w_ref[...], out_w_ref[...]

    def masked(values, mask):
        return jnp.where(mask, values, 0.0).astype(BF)

    def node_match(shape, hidden_axis):
        hidden = iota(shape, hidden_axis) >> 6
        return hidden == (iota(shape, 1 - hidden_axis) & 15)

    w1[...] = masked(mm(mm_nt(e1, in_wt).astype(BF), e2), node_match((1024, 256), 0))
    w1t[...] = masked(mm(mm(e2t, in_wt).astype(BF), e1t), node_match((256, 1024), 1))
    o16[...] = masked(mm(mm(e3t, out_w).astype(BF), e1t), node_match((128, 1024), 1))
    o16t[...] = masked(mm(mm_nt(e1, out_w).astype(BF), e3), node_match((1024, 128), 0))
    same = (iota((256, 256), 0) >> 6) == (iota((256, 256), 1) >> 6)
    m4[...] = masked(mm(mm(e1[:256], mid_w).astype(BF), e1t[:, :256]), same)
    m4t[...] = masked(mm(mm_nt(e1[:256], mid_w).astype(BF), e1t[:, :256]), same)
    bias1 = jnp.concatenate([in_b_ref[...]] * 4, axis=1)
    bias2 = jnp.concatenate([mid_b_ref[...]] * 4, axis=1)

    def group_rows(parts, width):
        blocks = []
        for g in range(4):
            picked = [
                part.reshape(5, 64, elements)[:, 16 * g : 16 * g + 16].reshape(80, elements)
                for part in parts
            ]
            padding = jnp.zeros((width - 80 * len(parts), elements), F32)
            blocks.append(jnp.transpose(jnp.concatenate(picked + [padding], axis=0)))
        return jnp.concatenate(blocks, axis=0).astype(BF)

    def ungroup(rows_ref, part):
        blocks = []
        for g in range(4):
            block = jnp.transpose(rows_ref[pl.ds(g * elements, elements), :])
            blocks.append(block[80 * part : 80 * part + 80].reshape(5, 16, elements))
        return jnp.concatenate(blocks, axis=1).reshape(320, elements)

    def columns_of(sub):
        return pl.ds(pl.multiple_of(sub * 256, 256), 256)

    def activations(sub):
        h1 = jnp.tanh(mm(x_in[...], w1t[:, columns_of(sub)]) + bias1)
        h2 = jnp.tanh(mm(h1.astype(BF), m4t[...]) + bias2)
        return h1, h2

    def back(sub, factor1, factor2):
        d2 = (mm(g_in[...], o16[:, columns_of(sub)]) * factor2).astype(BF)
        d1 = (mm(d2, m4[...]) * factor1).astype(BF)
        x_grad[...] += mm(d1, w1[columns_of(sub), :])

    volume0 = mm(vol_op_ref[...], field0)
    x_in[...] = group_rows([field0.astype(F32), volume0], 256)
    clo[...] = jnp.zeros_like(clo)

    def forward_step(sub, carry):
        h1, h2 = activations(sub)
        slope1[sub] = (1.0 - h1 * h1).astype(BF)
        slope2[sub] = (1.0 - h2 * h2).astype(BF)
        clo[...] += mm(h2.astype(BF), o16t[columns_of(sub), :])
        return carry

    lax.fori_loop(0, 4, forward_step, 0)
    base0 = w_ref[...] + time_step * (volume0 + ungroup(clo, 0))

    wait_exchange(0)
    jump = near[...] + pick_columns(got_forward(0), link_hot, link_high, 6)
    flux = mix(flux_ref, lift_gain * jump, False)
    middle = base0 + time_step * lift(face_t, to_tall(flux, elements))
    middle_s[...] = middle
    trace_grad = grad_near[...] + add_columns(
        got_backward(0), send_hot_t, send_high, 0, 6
    )
    adj_lift = lift(face_t, trace_grad)

    field1 = middle.astype(BF)
    traces1 = traces_of(field1)
    traces_s[...] = traces1
    put_forward(1, pick_columns(traces1, send_hot, send_high, 0))
    volume1 = mm(vol_op_ref[...], field1)
    x_in[...] = group_rows([field1.astype(F32), volume1], 256)
    g_in[...] = group_rows([ct_ref[...]], 128)
    clo[...] = jnp.zeros_like(clo)
    x_grad[...] = jnp.zeros_like(x_grad)

    def both_step(sub, carry):
        h1, h2 = activations(sub)
        clo[...] += mm(h2.astype(BF), o16t[columns_of(sub), :])
        back(sub, 1.0 - h1 * h1, 1.0 - h2 * h2)
        return carry

    lax.fori_loop(0, 4, both_step, 0)

    def input_part(adjoint):
        field_grad, volume_grad = ungroup(x_grad, 0), ungroup(x_grad, 1)
        return mm_tn(vol_op_ref[...], (adjoint + volume_grad).astype(BF)) + field_grad

    ct = ct_ref[...]
    adj_mid = 0.5 * ct + 0.5 * time_step * (input_part(ct) + adj_lift)
    adj_mid_s[...] = adj_mid
    jump1 = jump_grad_of(adj_mid)
    jump1_b = jump1.astype(BF)
    put_backward(1, add_columns(jump1_b, link_hot_t, link_high, 6, far_count))
    start_exchange(1)

    final_ref[...] = 0.5 * w_ref[...] + 0.5 * (
        middle_s[...] + time_step * (volume1 + ungroup(clo, 0))
    )
    near[...] = pick_columns(traces_s[...], link_hot, link_high, 0) - to_wide(
        traces_s[...].astype(F32), elements
    )
    grad_near[...] = add_columns(jump1_b, link_hot_t, link_high, 0, 6) - to_tall(
        jump1, elements
    )
    g_in[...] = group_rows([adj_mid], 128)
    x_grad[...] = jnp.zeros_like(x_grad)

    def back_step(sub, carry):
        back(sub, slope1[sub].astype(F32), slope2[sub].astype(F32))
        return carry

    lax.fori_loop(0, 4, back_step, 0)
    adj_mid = adj_mid_s[...]
    adj_ref[...] = 0.5 * ct_ref[...] + adj_mid + time_step * input_part(adj_mid)

    wait_exchange(1)
    jump = near[...] + pick_columns(got_forward(1), link_hot, link_high, 6)
    flux = mix(flux_ref, lift_gain * jump, False)
    final_ref[...] += 0.5 * time_step * lift(face_t, to_tall(flux, elements))
    trace_grad = grad_near[...] + add_columns(
        got_backward(1), send_hot_t, send_high, 0, 6
    )
    adj_ref[...] += time_step * lift(face_t, trace_grad)


def body(
    n_dom,
    n_sub,
    initial_state,
    cotangent,
    volume_operator,
    in_weight,
    in_bias,
    mid_weight,
    mid_bias,
    out_weight,
    flux_matrix,
    dom_send,
    dom_count,
    sub_send,
    partner,
):
    elements = initial_state.shape[1]
    faces = 6 * elements
    slots = dom_send.shape[1] + sub_send.shape[1]
    vmem = pl.BlockSpec(memory_space=pltpu.VMEM)
    smem = pl.BlockSpec(memory_space=pltpu.SMEM)
    state = jax.ShapeDtypeStruct(initial_state.shape, F32)
    return pl.pallas_call(
        functools.partial(kernel, n_dom, n_sub),
        out_shape=(state, state),
        in_specs=[vmem] * 8 + [smem, vmem, smem] + [vmem] * 2,
        out_specs=(vmem, vmem),
        scratch_shapes=[
            pltpu.VMEM((256, faces), BF),
            pltpu.VMEM((faces, 256), BF),
            pltpu.VMEM((256, slots), BF),
            pltpu.VMEM((slots, 256), BF),
            pltpu.VMEM((1024, 256), BF),
            pltpu.VMEM((256, 1024), BF),
            pltpu.VMEM((256, 256), BF),
            pltpu.VMEM((256, 256), BF),
            pltpu.VMEM((128, 1024), BF),
            pltpu.VMEM((1024, 128), BF),
            pltpu.VMEM((4 * elements, 256), BF),
            pltpu.VMEM((4 * elements, 128), BF),
            pltpu.VMEM((4 * elements, 128), F32),
            pltpu.VMEM((4 * elements, 256), F32),
            pltpu.VMEM((4, 4 * elements, 256), BF),
            pltpu.VMEM((4, 4 * elements, 256), BF),
            pltpu.VMEM((480, elements), BF),
            pltpu.VMEM((80, faces), F32),
            pltpu.VMEM((480, elements), F32),
            pltpu.VMEM(initial_state.shape, F32),
            pltpu.VMEM(initial_state.shape, F32),
            pltpu.VMEM((2, slots, 256), BF),
            pltpu.VMEM((2, slots, 256), BF),
            pltpu.SemaphoreType.DMA((2, PAIRS)),
            pltpu.SemaphoreType.DMA((2, PAIRS)),
            pltpu.SemaphoreType.DMA((2, n_sub - 1)),
            pltpu.SemaphoreType.DMA((2, n_sub - 1)),
        ],
        compiler_params=pltpu.CompilerParams(
            collective_id=0, has_side_effects=True, vmem_limit_bytes=56 * 1024 * 1024
        ),
        cost_estimate=pl.CostEstimate(
            flops=8_000_000_000, bytes_accessed=4_000_000, transcendentals=4_000_000
        ),
    )(
        initial_state,
        cotangent,
        volume_operator,
        in_weight.T,
        in_bias.reshape(1, -1),
        mid_weight,
        mid_bias.reshape(1, -1),
        out_weight,
        flux_matrix,
        dom_send,
        dom_count,
        sub_send,
        partner,
    )


def solution(mesh):
    return jax.shard_map(
        functools.partial(body, mesh.shape["dom"], mesh.shape["sub"]),
        mesh=mesh,
        in_specs=(
            P(None, ("dom", "sub")),
            P(None, ("dom", "sub")),
            P(),
            P(),
            P(),
            P(),
            P(),
            P(),
            P(),
            P("dom", "sub"),
            P("dom", "sub"),
            P("dom", "sub"),
            P("dom", "sub"),
        ),
        out_specs=(P(None, ("dom", "sub")), P(None, ("dom", "sub"))),
        check_vma=False,
    )
```

```python
import functools

import jax
import jax.numpy as jnp
from jax import lax
from jax.experimental import pallas as pl
from jax.experimental.pallas import tpu as pltpu
from jax.sharding import PartitionSpec as P

REACH = 4
OFFSETS = [offset for offset in range(-REACH, REACH + 1) if offset != 0]
PAIRS = len(OFFSETS)
MESH = pl.DeviceIdType.MESH

time_step = 0.4
lift_gain = 1.5
BF = jnp.bfloat16
F32 = jnp.float32


def iota(shape, axis):
    return lax.broadcasted_iota(jnp.int32, shape, axis)


def hot(mask):
    return jnp.where(mask, 1.0, 0.0).astype(BF)


def face_node(row):
    f = sum((row >= 80 * i).astype(jnp.int32) for i in range(1, 6))
    within = row - 80 * f
    v, k = within >> 4, within & 15
    end = f & 1
    node = jnp.where(
        f < 2,
        3 * end + 4 * k,
        jnp.where(f < 4, (k & 3) + 16 * (k >> 2) + 12 * end, k + 48 * end),
    )
    return 64 * v + node


def mm(a, b):
    return jnp.dot(a, b, preferred_element_type=F32)


def mm_nt(a, b):
    return lax.dot_general(a, b, (((1,), (1,)), ((), ())), preferred_element_type=F32)


def mm_tn(a, b):
    return lax.dot_general(a, b, (((0,), (0,)), ((), ())), preferred_element_type=F32)


def split(values):
    high = values.astype(BF)
    return high, (values - high.astype(F32)).astype(BF)


def to_wide(faces, elements):
    return jnp.concatenate([faces[f * 80 : (f + 1) * 80] for f in range(6)], axis=1)


def to_tall(wide, elements):
    return jnp.concatenate(
        [wide[:, f * elements : (f + 1) * elements] for f in range(6)], axis=0
    )


def lift(face_t, tall):
    high, low = split(tall)
    return mm(face_t, high) + mm(face_t, low)


def mix(flux_ref, values, transposed):
    rows = []
    for v in range(5):
        total = None
        for u in range(5):
            weight = flux_ref[u, v] if transposed else flux_ref[v, u]
            term = weight * values[u * 16 : (u + 1) * 16]
            total = term if total is None else total + term
        rows.append(total)
    return jnp.concatenate(rows, axis=0)


def one_hot_lanes(row_list):
    width = row_list.shape[1]
    low = jnp.broadcast_to(row_list & 255, (256, width))
    return jnp.where(low == iota((256, width), 0), 1.0, 0.0)


def pick_columns(blocks, low_hot, high, first):
    picked = []
    for base in range(0, high.shape[1], 256):
        products = mm(blocks, low_hot[:, base : base + 256])
        mine = high[:, base : base + 256]
        total = jnp.zeros((80, 256), F32)
        for b in range(blocks.shape[0] // 80):
            total = jnp.where(mine == first + b, products[b * 80 : (b + 1) * 80], total)
        picked.append(total)
    return jnp.concatenate(picked, axis=1)


def add_columns(values, low_hot_t, high, first, count):
    parts = [
        values * jnp.where(high == first + b, 1.0, 0.0).astype(BF) for b in range(count)
    ]
    return mm(jnp.concatenate(parts, axis=0), low_hot_t[...])


def kernel(
    n_dom,
    n_sub,
    w_ref,
    ct_ref,
    vol_op_ref,
    in_wt_ref,
    in_b_ref,
    mid_w_ref,
    mid_b_ref,
    out_w_ref,
    flux_ref,
    dom_ref,
    count_ref,
    sub_ref,
    partner_ref,
    final_ref,
    adj_ref,
    link_hot,
    link_hot_t,
    send_hot,
    send_hot_t,
    w1,
    w1t,
    m4,
    m4t,
    o16,
    o16t,
    x_in,
    g_in,
    clo,
    x_grad,
    slope1,
    slope2,
    traces_s,
    near,
    grad_near,
    middle_s,
    adj_mid_s,
    out_buf,
    in_buf,
    dom_send_sem,
    dom_recv_sem,
    sub_send_sem,
    sub_recv_sem,
):
    elements = w_ref.shape[1]
    faces = 6 * elements
    dom_width = dom_ref.shape[1]
    peer_slots = dom_width // PAIRS
    sub_width = sub_ref.shape[1]
    sub_slots = sub_width // n_sub
    slots = dom_width + sub_width
    d = lax.axis_index("dom")
    s = lax.axis_index("sub")

    def inside(j):
        target = d + OFFSETS[j]
        return (target >= 0) & (target < n_dom)

    barrier = pltpu.get_barrier_semaphore()
    expected = n_sub - 1
    for j in range(PAIRS):
        expected = expected + jnp.where(inside(j), 1, 0)

        @pl.when(inside(j))
        def _():
            pl.semaphore_signal(
                barrier, inc=1, device_id=(d + OFFSETS[j], s), device_id_type=MESH
            )

    for step in range(1, n_sub):
        pl.semaphore_signal(
            barrier, inc=1, device_id=(d, lax.rem(s + step, n_sub)), device_id_type=MESH
        )

    def dom_copy(phase, j):
        rows = pl.ds(j * peer_slots, peer_slots)
        return pltpu.make_async_remote_copy(
            src_ref=out_buf.at[phase, rows],
            dst_ref=in_buf.at[phase, rows],
            send_sem=dom_send_sem.at[phase, j],
            recv_sem=dom_recv_sem.at[phase, j],
            device_id=(d + OFFSETS[j], s),
            device_id_type=MESH,
        )

    def sub_copy(phase, step):
        there = lax.rem(s + step, n_sub)
        source = pl.ds(pl.multiple_of(dom_width + there * sub_slots, 32), sub_slots)
        target = pl.ds(pl.multiple_of(dom_width + s * sub_slots, 32), sub_slots)
        return pltpu.make_async_remote_copy(
            src_ref=out_buf.at[phase, source],
            dst_ref=in_buf.at[phase, target],
            send_sem=sub_send_sem.at[phase, step - 1],
            recv_sem=sub_recv_sem.at[phase, step - 1],
            device_id=(d, there),
            device_id_type=MESH,
        )

    def start_exchange(phase):
        for j in range(PAIRS):

            @pl.when(inside(j))
            def _():
                dom_copy(phase, j).start()

        for step in range(1, n_sub):
            sub_copy(phase, step).start()
        own = pl.ds(pl.multiple_of(dom_width + s * sub_slots, 32), sub_slots)
        in_buf[phase, own, :] = out_buf[phase, own, :]

    def wait_exchange(phase):
        for j in range(PAIRS):
            @pl.when(inside(PAIRS - 1 - j))
            def _():
                dom_copy(phase, j).wait_recv()

            @pl.when(inside(j))
            def _():
                dom_copy(phase, j).wait_send()

            @pl.when(jnp.logical_not(inside(PAIRS - 1 - j)))
            def _():
                in_buf[phase, pl.ds(j * peer_slots, peer_slots), :] = jnp.zeros(
                    (peer_slots, 256), BF
                )

        for step in range(1, n_sub):
            sub_copy(phase, step).wait()

    def flip(rows):
        parts = [
            rows[j * peer_slots : (j + 1) * peer_slots] for j in reversed(range(PAIRS))
        ]
        return jnp.concatenate(parts + [rows[dom_width:]], axis=0)

    def put_forward(phase, values):
        out_buf[phase, :, 0:128] = to_rows(values).astype(BF)

    def to_rows(values):
        padding = jnp.zeros((48, values.shape[1]), F32)
        return jnp.transpose(jnp.concatenate([values, padding], axis=0))

    def put_backward(phase, blocks):
        wide = jnp.concatenate(
            [blocks[80 * b : 80 * b + 80] for b in range(slots // 256)], axis=1
        )
        out_buf[phase, :, 128:256] = flip(to_rows(wide)).astype(BF)

    def got_forward(phase):
        wide = jnp.transpose(in_buf[phase, :, 0:128].astype(F32))[:80].astype(BF)
        return jnp.concatenate([wide[:, b : b + 256] for b in range(0, slots, 256)], axis=0)

    def got_backward(phase):
        rows = flip(in_buf[phase, :, 128:256].astype(F32))
        return jnp.transpose(rows)[:80].astype(BF)

    lane = lax.broadcasted_iota(jnp.int32, (1, dom_width), 1)
    dom_list = dom_ref[...]
    for j in range(PAIRS):
        dead = (lane >= j * peer_slots + count_ref[0, j]) & (lane < (j + 1) * peer_slots)
        dom_list = jnp.where(dead, -1, dom_list)
    send_list = jnp.concatenate([dom_list, sub_ref[...]], axis=1)
    send_low = one_hot_lanes(send_list)
    send_hot[...] = send_low.astype(BF)
    send_hot_t[...] = jnp.transpose(send_low).astype(BF)
    send_high = send_list >> 8
    partner = partner_ref[...]
    link_low = one_hot_lanes(partner)
    link_hot[...] = link_low.astype(BF)
    link_hot_t[...] = jnp.transpose(link_low).astype(BF)
    link_high = partner >> 8
    far_count = slots // 256

    face = hot(iota((480, 320), 1) == face_node(iota((480, 1), 0)))
    face_t = hot(iota((320, 480), 0) == face_node(iota((1, 480), 1)))

    def traces_of(field_b):
        return mm(face, field_b).astype(BF)

    def jump_grad_of(g):
        high, low = split(g)
        values = to_wide(mm(face, high) + mm(face, low), elements)
        return mix(flux_ref, lift_gain * values, True)

    field0 = w_ref[...].astype(BF)
    traces0 = traces_of(field0)
    put_forward(0, pick_columns(traces0, send_hot, send_high, 0))
    jump0 = jump_grad_of(ct_ref[...])
    jump0_b = jump0.astype(BF)
    put_backward(0, add_columns(jump0_b, link_hot_t, link_high, 6, far_count))
    pl.semaphore_wait(barrier, expected)
    start_exchange(0)

    near[...] = pick_columns(traces0, link_hot, link_high, 0) - to_wide(
        traces0.astype(F32), elements
    )
    grad_near[...] = add_columns(jump0_b, link_hot_t, link_high, 0, 6) - to_tall(
        jump0, elements
    )

    e1 = hot((iota((1024, 64), 0) & 63) == iota((1024, 64), 1))
    e1t = hot((iota((64, 1024), 1) & 63) == iota((64, 1024), 0))
    e2 = hot((iota((10, 256), 1) >> 4) == iota((10, 256), 0))
    e2t = hot((iota((256, 10), 0) >> 4) == iota((256, 10), 1))
    e3 = hot((iota((5, 128), 1) >> 4) == iota((5, 128), 0))
    e3t = hot((iota((128, 5), 0) >> 4) == iota((128, 5), 1))
    in_wt, mid_w, out_w = in_wt_ref[...], mid_w_ref[...], out_w_ref[...]

    def masked(values, mask):
        return jnp.where(mask, values, 0.0).astype(BF)

    def node_match(shape, hidden_axis):
        hidden = iota(shape, hidden_axis) >> 6
        return hidden == (iota(shape, 1 - hidden_axis) & 15)

    w1[...] = masked(mm(mm_nt(e1, in_wt).astype(BF), e2), node_match((1024, 256), 0))
    w1t[...] = masked(mm(mm(e2t, in_wt).astype(BF), e1t), node_match((256, 1024), 1))
    o16[...] = masked(mm(mm(e3t, out_w).astype(BF), e1t), node_match((128, 1024), 1))
    o16t[...] = masked(mm(mm_nt(e1, out_w).astype(BF), e3), node_match((1024, 128), 0))
    same = (iota((256, 256), 0) >> 6) == (iota((256, 256), 1) >> 6)
    m4[...] = masked(mm(mm(e1[:256], mid_w).astype(BF), e1t[:, :256]), same)
    m4t[...] = masked(mm(mm_nt(e1[:256], mid_w).astype(BF), e1t[:, :256]), same)
    bias1 = jnp.concatenate([in_b_ref[...]] * 4, axis=1)
    bias2 = jnp.concatenate([mid_b_ref[...]] * 4, axis=1)

    def group_rows(parts, width):
        blocks = []
        for g in range(4):
            picked = [
                part.reshape(5, 64, elements)[:, 16 * g : 16 * g + 16].reshape(80, elements)
                for part in parts
            ]
            padding = jnp.zeros((width - 80 * len(parts), elements), F32)
            blocks.append(jnp.transpose(jnp.concatenate(picked + [padding], axis=0)))
        return jnp.concatenate(blocks, axis=0).astype(BF)

    def ungroup(rows_ref, part):
        blocks = []
        for g in range(4):
            block = jnp.transpose(rows_ref[pl.ds(g * elements, elements), :])
            blocks.append(block[80 * part : 80 * part + 80].reshape(5, 16, elements))
        return jnp.concatenate(blocks, axis=1).reshape(320, elements)

    def columns_of(sub):
        return pl.ds(pl.multiple_of(sub * 256, 256), 256)

    def activations(sub):
        h1 = jnp.tanh(mm(x_in[...], w1t[:, columns_of(sub)]) + bias1)
        h2 = jnp.tanh(mm(h1.astype(BF), m4t[...]) + bias2)
        return h1, h2

    def back(sub, factor1, factor2):
        d2 = (mm(g_in[...], o16[:, columns_of(sub)]) * factor2).astype(BF)
        d1 = (mm(d2, m4[...]) * factor1).astype(BF)
        x_grad[...] += mm(d1, w1[columns_of(sub), :])

    volume0 = mm(vol_op_ref[...], field0)
    x_in[...] = group_rows([field0.astype(F32), volume0], 256)
    clo[...] = jnp.zeros_like(clo)

    def forward_step(sub, carry):
        h1, h2 = activations(sub)
        slope1[sub] = (1.0 - h1 * h1).astype(BF)
        slope2[sub] = (1.0 - h2 * h2).astype(BF)
        clo[...] += mm(h2.astype(BF), o16t[columns_of(sub), :])
        return carry

    lax.fori_loop(0, 4, forward_step, 0, unroll=True)
    base0 = w_ref[...] + time_step * (volume0 + ungroup(clo, 0))

    wait_exchange(0)
    jump = near[...] + pick_columns(got_forward(0), link_hot, link_high, 6)
    flux = mix(flux_ref, lift_gain * jump, False)
    middle = base0 + time_step * lift(face_t, to_tall(flux, elements))
    middle_s[...] = middle
    trace_grad = grad_near[...] + add_columns(
        got_backward(0), send_hot_t, send_high, 0, 6
    )
    adj_lift = lift(face_t, trace_grad)

    field1 = middle.astype(BF)
    traces1 = traces_of(field1)
    traces_s[...] = traces1
    put_forward(1, pick_columns(traces1, send_hot, send_high, 0))
    volume1 = mm(vol_op_ref[...], field1)
    x_in[...] = group_rows([field1.astype(F32), volume1], 256)
    g_in[...] = group_rows([ct_ref[...]], 128)
    clo[...] = jnp.zeros_like(clo)
    x_grad[...] = jnp.zeros_like(x_grad)

    def both_step(sub, carry):
        h1, h2 = activations(sub)
        clo[...] += mm(h2.astype(BF), o16t[columns_of(sub), :])
        back(sub, 1.0 - h1 * h1, 1.0 - h2 * h2)
        return carry

    lax.fori_loop(0, 4, both_step, 0, unroll=True)

    def input_part(adjoint):
        field_grad, volume_grad = ungroup(x_grad, 0), ungroup(x_grad, 1)
        return mm_tn(vol_op_ref[...], (adjoint + volume_grad).astype(BF)) + field_grad

    ct = ct_ref[...]
    adj_mid = 0.5 * ct + 0.5 * time_step * (input_part(ct) + adj_lift)
    adj_mid_s[...] = adj_mid
    jump1 = jump_grad_of(adj_mid)
    jump1_b = jump1.astype(BF)
    put_backward(1, add_columns(jump1_b, link_hot_t, link_high, 6, far_count))
    start_exchange(1)

    final_ref[...] = 0.5 * w_ref[...] + 0.5 * (
        middle_s[...] + time_step * (volume1 + ungroup(clo, 0))
    )
    near[...] = pick_columns(traces_s[...], link_hot, link_high, 0) - to_wide(
        traces_s[...].astype(F32), elements
    )
    grad_near[...] = add_columns(jump1_b, link_hot_t, link_high, 0, 6) - to_tall(
        jump1, elements
    )
    g_in[...] = group_rows([adj_mid], 128)
    x_grad[...] = jnp.zeros_like(x_grad)

    def back_step(sub, carry):
        back(sub, slope1[sub].astype(F32), slope2[sub].astype(F32))
        return carry

    lax.fori_loop(0, 4, back_step, 0, unroll=True)
    adj_mid = adj_mid_s[...]
    adj_ref[...] = 0.5 * ct_ref[...] + adj_mid + time_step * input_part(adj_mid)

    wait_exchange(1)
    jump = near[...] + pick_columns(got_forward(1), link_hot, link_high, 6)
    flux = mix(flux_ref, lift_gain * jump, False)
    final_ref[...] += 0.5 * time_step * lift(face_t, to_tall(flux, elements))
    trace_grad = grad_near[...] + add_columns(
        got_backward(1), send_hot_t, send_high, 0, 6
    )
    adj_ref[...] += time_step * lift(face_t, trace_grad)


def hand_over(final_ref, adj_ref, final_out, adj_out, sems):
    half = final_ref.shape[0] // 2
    copies = []
    for i, (source, target) in enumerate(((final_ref, final_out), (adj_ref, adj_out))):
        for part in range(2):
            rows = pl.ds(part * half, half)
            copies.append(
                pltpu.make_async_copy(
                    source.at[rows], target.at[rows], sems.at[2 * i + part]
                )
            )
    for copy in copies:
        copy.start()
    for copy in copies:
        copy.wait()


def body(
    n_dom,
    n_sub,
    initial_state,
    cotangent,
    volume_operator,
    in_weight,
    in_bias,
    mid_weight,
    mid_bias,
    out_weight,
    flux_matrix,
    dom_send,
    dom_count,
    sub_send,
    partner,
):
    elements = initial_state.shape[1]
    faces = 6 * elements
    slots = dom_send.shape[1] + sub_send.shape[1]
    vmem = pl.BlockSpec(memory_space=pltpu.VMEM)
    smem = pl.BlockSpec(memory_space=pltpu.SMEM)
    state = jax.ShapeDtypeStruct(initial_state.shape, F32)
    results = pl.pallas_call(
        functools.partial(kernel, n_dom, n_sub),
        out_shape=(state, state),
        in_specs=[vmem] * 8 + [smem, vmem, smem] + [vmem] * 2,
        out_specs=(vmem, vmem),
        scratch_shapes=[
            pltpu.VMEM((256, faces), BF),
            pltpu.VMEM((faces, 256), BF),
            pltpu.VMEM((256, slots), BF),
            pltpu.VMEM((slots, 256), BF),
            pltpu.VMEM((1024, 256), BF),
            pltpu.VMEM((256, 1024), BF),
            pltpu.VMEM((256, 256), BF),
            pltpu.VMEM((256, 256), BF),
            pltpu.VMEM((128, 1024), BF),
            pltpu.VMEM((1024, 128), BF),
            pltpu.VMEM((4 * elements, 256), BF),
            pltpu.VMEM((4 * elements, 128), BF),
            pltpu.VMEM((4 * elements, 128), F32),
            pltpu.VMEM((4 * elements, 256), F32),
            pltpu.VMEM((4, 4 * elements, 256), BF),
            pltpu.VMEM((4, 4 * elements, 256), BF),
            pltpu.VMEM((480, elements), BF),
            pltpu.VMEM((80, faces), F32),
            pltpu.VMEM((480, elements), F32),
            pltpu.VMEM(initial_state.shape, F32),
            pltpu.VMEM(initial_state.shape, F32),
            pltpu.VMEM((2, slots, 256), BF),
            pltpu.VMEM((2, slots, 256), BF),
            pltpu.SemaphoreType.DMA((2, PAIRS)),
            pltpu.SemaphoreType.DMA((2, PAIRS)),
            pltpu.SemaphoreType.DMA((2, n_sub - 1)),
            pltpu.SemaphoreType.DMA((2, n_sub - 1)),
        ],
        compiler_params=pltpu.CompilerParams(
            collective_id=0, has_side_effects=True, vmem_limit_bytes=56 * 1024 * 1024
        ),
        cost_estimate=pl.CostEstimate(
            flops=8_000_000_000, bytes_accessed=4_000_000, transcendentals=4_000_000
        ),
    )(
        initial_state,
        cotangent,
        volume_operator,
        in_weight.T,
        in_bias.reshape(1, -1),
        mid_weight,
        mid_bias.reshape(1, -1),
        out_weight,
        flux_matrix,
        dom_send,
        dom_count,
        sub_send,
        partner,
    )

    return pl.pallas_call(
        hand_over,
        out_shape=(state, state),
        in_specs=[pl.BlockSpec(memory_space=pl.ANY)] * 2,
        out_specs=(pl.BlockSpec(memory_space=pl.ANY),) * 2,
        scratch_shapes=[pltpu.SemaphoreType.DMA((4,))],
        compiler_params=pltpu.CompilerParams(vmem_limit_bytes=56 * 1024 * 1024),
    )(*results)


def solution(mesh):
    return jax.shard_map(
        functools.partial(body, mesh.shape["dom"], mesh.shape["sub"]),
        mesh=mesh,
        in_specs=(
            P(None, ("dom", "sub")),
            P(None, ("dom", "sub")),
            P(),
            P(),
            P(),
            P(),
            P(),
            P(),
            P(),
            P("dom", "sub"),
            P("dom", "sub"),
            P("dom", "sub"),
            P("dom", "sub"),
        ),
        out_specs=(P(None, ("dom", "sub")), P(None, ("dom", "sub"))),
        check_vma=False,
    )
```

```python
import functools

import jax
import jax.numpy as jnp
from jax import lax
from jax.experimental import pallas as pl
from jax.experimental.pallas import tpu as pltpu
from jax.sharding import PartitionSpec as P

REACH = 4
OFFSETS = [offset for offset in range(-REACH, REACH + 1) if offset != 0]
PAIRS = len(OFFSETS)
MESH = pl.DeviceIdType.MESH

time_step = 0.4
lift_gain = 1.5
BF = jnp.bfloat16
F32 = jnp.float32


def iota(shape, axis):
    return lax.broadcasted_iota(jnp.int32, shape, axis)


def hot(mask):
    return jnp.where(mask, 1.0, 0.0).astype(BF)


def face_node(row):
    f = sum((row >= 80 * i).astype(jnp.int32) for i in range(1, 6))
    within = row - 80 * f
    v, k = within >> 4, within & 15
    end = f & 1
    node = jnp.where(
        f < 2,
        3 * end + 4 * k,
        jnp.where(f < 4, (k & 3) + 16 * (k >> 2) + 12 * end, k + 48 * end),
    )
    return 64 * v + node


def mm(a, b):
    return jnp.dot(a, b, preferred_element_type=F32)


def mm_nt(a, b):
    return lax.dot_general(a, b, (((1,), (1,)), ((), ())), preferred_element_type=F32)


def mm_tn(a, b):
    return lax.dot_general(a, b, (((0,), (0,)), ((), ())), preferred_element_type=F32)


def split(values):
    high = values.astype(BF)
    return high, (values - high.astype(F32)).astype(BF)


def to_wide(faces, elements):
    return jnp.concatenate([faces[f * 80 : (f + 1) * 80] for f in range(6)], axis=1)


def to_tall(wide, elements):
    return jnp.concatenate(
        [wide[:, f * elements : (f + 1) * elements] for f in range(6)], axis=0
    )


def lift(face_t, tall):
    high, low = split(tall)
    return mm(face_t, high) + mm(face_t, low)


def mix(flux_ref, values, transposed):
    rows = []
    for v in range(5):
        total = None
        for u in range(5):
            weight = flux_ref[u, v] if transposed else flux_ref[v, u]
            term = weight * values[u * 16 : (u + 1) * 16]
            total = term if total is None else total + term
        rows.append(total)
    return jnp.concatenate(rows, axis=0)


def one_hot_lanes(row_list):
    width = row_list.shape[1]
    low = jnp.broadcast_to(row_list & 255, (256, width))
    return jnp.where(low == iota((256, width), 0), 1.0, 0.0)


def pick_columns(blocks, low_hot, high, first):
    picked = []
    for base in range(0, high.shape[1], 256):
        products = mm(blocks, low_hot[:, base : base + 256])
        mine = high[:, base : base + 256]
        total = jnp.zeros((80, 256), F32)
        for b in range(blocks.shape[0] // 80):
            total = jnp.where(mine == first + b, products[b * 80 : (b + 1) * 80], total)
        picked.append(total)
    return jnp.concatenate(picked, axis=1)


def add_columns(values, low_hot_t, high, first, count):
    parts = [
        values * jnp.where(high == first + b, 1.0, 0.0).astype(BF) for b in range(count)
    ]
    return mm(jnp.concatenate(parts, axis=0), low_hot_t[...])


def kernel(
    n_dom,
    n_sub,
    w_ref,
    ct_ref,
    vol_op_ref,
    in_wt_ref,
    in_b_ref,
    mid_w_ref,
    mid_b_ref,
    out_w_ref,
    flux_ref,
    dom_ref,
    count_ref,
    sub_ref,
    partner_ref,
    final_ref,
    adj_ref,
    link_hot,
    link_hot_t,
    send_hot,
    send_hot_t,
    w1,
    w1t,
    m4,
    m4t,
    o16,
    o16t,
    x_in,
    g_in,
    clo,
    x_grad,
    slope1,
    slope2,
    traces_s,
    near,
    grad_near,
    middle_s,
    adj_mid_s,
    out_buf,
    in_buf,
    dom_send_sem,
    dom_recv_sem,
    sub_send_sem,
    sub_recv_sem,
):
    elements = w_ref.shape[1]
    faces = 6 * elements
    dom_width = dom_ref.shape[1]
    peer_slots = dom_width // PAIRS
    sub_width = sub_ref.shape[1]
    sub_slots = sub_width // n_sub
    slots = dom_width + sub_width
    d = lax.axis_index("dom")
    s = lax.axis_index("sub")

    def inside(j):
        target = d + OFFSETS[j]
        return (target >= 0) & (target < n_dom)

    barrier = pltpu.get_barrier_semaphore()
    expected = n_sub - 1
    for j in range(PAIRS):
        expected = expected + jnp.where(inside(j), 1, 0)

        @pl.when(inside(j))
        def _():
            pl.semaphore_signal(
                barrier, inc=1, device_id=(d + OFFSETS[j], s), device_id_type=MESH
            )

    for step in range(1, n_sub):
        pl.semaphore_signal(
            barrier, inc=1, device_id=(d, lax.rem(s + step, n_sub)), device_id_type=MESH
        )

    def dom_copy(phase, j):
        rows = pl.ds(j * peer_slots, peer_slots)
        return pltpu.make_async_remote_copy(
            src_ref=out_buf.at[phase, rows],
            dst_ref=in_buf.at[phase, rows],
            send_sem=dom_send_sem.at[phase, j],
            recv_sem=dom_recv_sem.at[phase, j],
            device_id=(d + OFFSETS[j], s),
            device_id_type=MESH,
        )

    def sub_copy(phase, step):
        there = lax.rem(s + step, n_sub)
        source = pl.ds(pl.multiple_of(dom_width + there * sub_slots, 32), sub_slots)
        target = pl.ds(pl.multiple_of(dom_width + s * sub_slots, 32), sub_slots)
        return pltpu.make_async_remote_copy(
            src_ref=out_buf.at[phase, source],
            dst_ref=in_buf.at[phase, target],
            send_sem=sub_send_sem.at[phase, step - 1],
            recv_sem=sub_recv_sem.at[phase, step - 1],
            device_id=(d, there),
            device_id_type=MESH,
        )

    def start_exchange(phase):
        for j in range(PAIRS):

            @pl.when(inside(j))
            def _():
                dom_copy(phase, j).start()

        for step in range(1, n_sub):
            sub_copy(phase, step).start()
        own = pl.ds(pl.multiple_of(dom_width + s * sub_slots, 32), sub_slots)
        in_buf[phase, own, :] = out_buf[phase, own, :]

    def wait_exchange(phase):
        for j in range(PAIRS):
            @pl.when(inside(PAIRS - 1 - j))
            def _():
                dom_copy(phase, j).wait_recv()

            @pl.when(inside(j))
            def _():
                dom_copy(phase, j).wait_send()

            @pl.when(jnp.logical_not(inside(PAIRS - 1 - j)))
            def _():
                in_buf[phase, pl.ds(j * peer_slots, peer_slots), :] = jnp.zeros(
                    (peer_slots, 256), BF
                )

        for step in range(1, n_sub):
            sub_copy(phase, step).wait()

    def flip(rows):
        parts = [
            rows[j * peer_slots : (j + 1) * peer_slots] for j in reversed(range(PAIRS))
        ]
        return jnp.concatenate(parts + [rows[dom_width:]], axis=0)

    def put_forward(phase, values):
        out_buf[phase, :, 0:128] = to_rows(values).astype(BF)

    def to_rows(values):
        padding = jnp.zeros((48, values.shape[1]), F32)
        return jnp.transpose(jnp.concatenate([values, padding], axis=0))

    def put_backward(phase, blocks):
        wide = jnp.concatenate(
            [blocks[80 * b : 80 * b + 80] for b in range(slots // 256)], axis=1
        )
        out_buf[phase, :, 128:256] = flip(to_rows(wide)).astype(BF)

    def got_forward(phase):
        wide = jnp.transpose(in_buf[phase, :, 0:128].astype(F32))[:80].astype(BF)
        return jnp.concatenate([wide[:, b : b + 256] for b in range(0, slots, 256)], axis=0)

    def got_backward(phase):
        rows = flip(in_buf[phase, :, 128:256].astype(F32))
        return jnp.transpose(rows)[:80].astype(BF)

    lane = lax.broadcasted_iota(jnp.int32, (1, dom_width), 1)
    dom_list = dom_ref[...]
    for j in range(PAIRS):
        dead = (lane >= j * peer_slots + count_ref[0, j]) & (lane < (j + 1) * peer_slots)
        dom_list = jnp.where(dead, -1, dom_list)
    send_list = jnp.concatenate([dom_list, sub_ref[...]], axis=1)
    send_low = one_hot_lanes(send_list)
    send_hot[...] = send_low.astype(BF)
    send_hot_t[...] = jnp.transpose(send_low).astype(BF)
    send_high = send_list >> 8
    partner = partner_ref[...]
    link_low = one_hot_lanes(partner)
    link_hot[...] = link_low.astype(BF)
    link_hot_t[...] = jnp.transpose(link_low).astype(BF)
    link_high = partner >> 8
    far_count = slots // 256

    face = hot(iota((480, 320), 1) == face_node(iota((480, 1), 0)))
    face_t = hot(iota((320, 480), 0) == face_node(iota((1, 480), 1)))

    def traces_of(field_b):
        return mm(face, field_b).astype(BF)

    def jump_grad_of(g):
        high, low = split(g)
        values = to_wide(mm(face, high) + mm(face, low), elements)
        return mix(flux_ref, lift_gain * values, True)

    field0 = w_ref[...].astype(BF)
    traces0 = traces_of(field0)
    put_forward(0, pick_columns(traces0, send_hot, send_high, 0))
    jump0 = jump_grad_of(ct_ref[...])
    jump0_b = jump0.astype(BF)
    put_backward(0, add_columns(jump0_b, link_hot_t, link_high, 6, far_count))
    pl.semaphore_wait(barrier, expected)
    start_exchange(0)

    near[...] = pick_columns(traces0, link_hot, link_high, 0) - to_wide(
        traces0.astype(F32), elements
    )
    grad_near[...] = add_columns(jump0_b, link_hot_t, link_high, 0, 6) - to_tall(
        jump0, elements
    )

    e1 = hot((iota((1024, 64), 0) & 63) == iota((1024, 64), 1))
    e1t = hot((iota((64, 1024), 1) & 63) == iota((64, 1024), 0))
    e2 = hot((iota((10, 256), 1) >> 4) == iota((10, 256), 0))
    e2t = hot((iota((256, 10), 0) >> 4) == iota((256, 10), 1))
    e3 = hot((iota((5, 128), 1) >> 4) == iota((5, 128), 0))
    e3t = hot((iota((128, 5), 0) >> 4) == iota((128, 5), 1))
    in_wt, mid_w, out_w = in_wt_ref[...], mid_w_ref[...], out_w_ref[...]

    def masked(values, mask):
        return jnp.where(mask, values, 0.0).astype(BF)

    def node_match(shape, hidden_axis):
        hidden = iota(shape, hidden_axis) >> 6
        return hidden == (iota(shape, 1 - hidden_axis) & 15)

    w1[...] = masked(mm(mm_nt(e1, in_wt).astype(BF), e2), node_match((1024, 256), 0))
    w1t[...] = masked(mm(mm(e2t, in_wt).astype(BF), e1t), node_match((256, 1024), 1))
    o16[...] = masked(mm(mm(e3t, out_w).astype(BF), e1t), node_match((128, 1024), 1))
    o16t[...] = masked(mm(mm_nt(e1, out_w).astype(BF), e3), node_match((1024, 128), 0))
    same = (iota((256, 256), 0) >> 6) == (iota((256, 256), 1) >> 6)
    m4[...] = masked(mm(mm(e1[:256], mid_w).astype(BF), e1t[:, :256]), same)
    m4t[...] = masked(mm(mm_nt(e1[:256], mid_w).astype(BF), e1t[:, :256]), same)
    bias1 = jnp.concatenate([in_b_ref[...]] * 4, axis=1)
    bias2 = jnp.concatenate([mid_b_ref[...]] * 4, axis=1)

    def group_rows(parts, width):
        blocks = []
        for g in range(4):
            picked = [
                part.reshape(5, 64, elements)[:, 16 * g : 16 * g + 16].reshape(80, elements)
                for part in parts
            ]
            padding = jnp.zeros((width - 80 * len(parts), elements), F32)
            blocks.append(jnp.transpose(jnp.concatenate(picked + [padding], axis=0)))
        return jnp.concatenate(blocks, axis=0).astype(BF)

    def ungroup(rows_ref, part):
        blocks = []
        for g in range(4):
            block = jnp.transpose(rows_ref[pl.ds(g * elements, elements), :])
            blocks.append(block[80 * part : 80 * part + 80].reshape(5, 16, elements))
        return jnp.concatenate(blocks, axis=1).reshape(320, elements)

    def columns_of(sub):
        return pl.ds(pl.multiple_of(sub * 256, 256), 256)

    def activations(sub):
        h1 = jnp.tanh(mm(x_in[...], w1t[:, columns_of(sub)]) + bias1)
        h2 = jnp.tanh(mm(h1.astype(BF), m4t[...]) + bias2)
        return h1, h2

    def back(sub, factor1, factor2):
        d2 = (mm(g_in[...], o16[:, columns_of(sub)]) * factor2).astype(BF)
        d1 = (mm(d2, m4[...]) * factor1).astype(BF)
        x_grad[...] += mm(d1, w1[columns_of(sub), :])

    volume0 = mm(vol_op_ref[...], field0)
    x_in[...] = group_rows([field0.astype(F32), volume0], 256)
    clo[...] = jnp.zeros_like(clo)

    def forward_step(sub, carry):
        h1, h2 = activations(sub)
        slope1[sub] = (1.0 - h1 * h1).astype(BF)
        slope2[sub] = (1.0 - h2 * h2).astype(BF)
        clo[...] += mm(h2.astype(BF), o16t[columns_of(sub), :])
        return carry

    lax.fori_loop(0, 4, forward_step, 0, unroll=True)
    base0 = w_ref[...] + time_step * (volume0 + ungroup(clo, 0))

    wait_exchange(0)
    jump = near[...] + pick_columns(got_forward(0), link_hot, link_high, 6)
    flux = mix(flux_ref, lift_gain * jump, False)
    middle = base0 + time_step * lift(face_t, to_tall(flux, elements))
    middle_s[...] = middle
    trace_grad = grad_near[...] + add_columns(
        got_backward(0), send_hot_t, send_high, 0, 6
    )
    adj_lift = lift(face_t, trace_grad)

    field1 = middle.astype(BF)
    traces1 = traces_of(field1)
    traces_s[...] = traces1
    put_forward(1, pick_columns(traces1, send_hot, send_high, 0))
    volume1 = mm(vol_op_ref[...], field1)
    x_in[...] = group_rows([field1.astype(F32), volume1], 256)
    g_in[...] = group_rows([ct_ref[...]], 128)
    clo[...] = jnp.zeros_like(clo)
    x_grad[...] = jnp.zeros_like(x_grad)

    def both_step(sub, carry):
        h1, h2 = activations(sub)
        clo[...] += mm(h2.astype(BF), o16t[columns_of(sub), :])
        back(sub, 1.0 - h1 * h1, 1.0 - h2 * h2)
        return carry

    lax.fori_loop(0, 4, both_step, 0, unroll=True)

    def input_part(adjoint):
        field_grad, volume_grad = ungroup(x_grad, 0), ungroup(x_grad, 1)
        return mm_tn(vol_op_ref[...], (adjoint + volume_grad).astype(BF)) + field_grad

    ct = ct_ref[...]
    adj_mid = 0.5 * ct + 0.5 * time_step * (input_part(ct) + adj_lift)
    adj_mid_s[...] = adj_mid
    jump1 = jump_grad_of(adj_mid)
    jump1_b = jump1.astype(BF)
    put_backward(1, add_columns(jump1_b, link_hot_t, link_high, 6, far_count))
    start_exchange(1)

    final_ref[...] = 0.5 * w_ref[...] + 0.5 * (
        middle_s[...] + time_step * (volume1 + ungroup(clo, 0))
    )
    near[...] = pick_columns(traces_s[...], link_hot, link_high, 0) - to_wide(
        traces_s[...].astype(F32), elements
    )
    grad_near[...] = add_columns(jump1_b, link_hot_t, link_high, 0, 6) - to_tall(
        jump1, elements
    )
    g_in[...] = group_rows([adj_mid], 128)
    x_grad[...] = jnp.zeros_like(x_grad)

    def back_step(sub, carry):
        back(sub, slope1[sub].astype(F32), slope2[sub].astype(F32))
        return carry

    lax.fori_loop(0, 4, back_step, 0, unroll=True)
    adj_mid = adj_mid_s[...]
    adj_ref[...] = 0.5 * ct_ref[...] + adj_mid + time_step * input_part(adj_mid)

    wait_exchange(1)
    jump = near[...] + pick_columns(got_forward(1), link_hot, link_high, 6)
    flux = mix(flux_ref, lift_gain * jump, False)
    final_ref[...] += 0.5 * time_step * lift(face_t, to_tall(flux, elements))
    trace_grad = grad_near[...] + add_columns(
        got_backward(1), send_hot_t, send_high, 0, 6
    )
    adj_ref[...] += time_step * lift(face_t, trace_grad)


def body(
    n_dom,
    n_sub,
    initial_state,
    cotangent,
    volume_operator,
    in_weight,
    in_bias,
    mid_weight,
    mid_bias,
    out_weight,
    flux_matrix,
    dom_send,
    dom_count,
    sub_send,
    partner,
):
    elements = initial_state.shape[1]
    faces = 6 * elements
    slots = dom_send.shape[1] + sub_send.shape[1]
    vmem = pl.BlockSpec(memory_space=pltpu.VMEM)
    smem = pl.BlockSpec(memory_space=pltpu.SMEM)
    state = jax.ShapeDtypeStruct(initial_state.shape, F32)
    return pl.pallas_call(
        functools.partial(kernel, n_dom, n_sub),
        out_shape=(state, state),
        in_specs=[vmem] * 8 + [smem, vmem, smem] + [vmem] * 2,
        out_specs=(vmem, vmem),
        scratch_shapes=[
            pltpu.VMEM((256, faces), BF),
            pltpu.VMEM((faces, 256), BF),
            pltpu.VMEM((256, slots), BF),
            pltpu.VMEM((slots, 256), BF),
            pltpu.VMEM((1024, 256), BF),
            pltpu.VMEM((256, 1024), BF),
            pltpu.VMEM((256, 256), BF),
            pltpu.VMEM((256, 256), BF),
            pltpu.VMEM((128, 1024), BF),
            pltpu.VMEM((1024, 128), BF),
            pltpu.VMEM((4 * elements, 256), BF),
            pltpu.VMEM((4 * elements, 128), BF),
            pltpu.VMEM((4 * elements, 128), F32),
            pltpu.VMEM((4 * elements, 256), F32),
            pltpu.VMEM((4, 4 * elements, 256), BF),
            pltpu.VMEM((4, 4 * elements, 256), BF),
            pltpu.VMEM((480, elements), BF),
            pltpu.VMEM((80, faces), F32),
            pltpu.VMEM((480, elements), F32),
            pltpu.VMEM(initial_state.shape, F32),
            pltpu.VMEM(initial_state.shape, F32),
            pltpu.VMEM((2, slots, 256), BF),
            pltpu.VMEM((2, slots, 256), BF),
            pltpu.SemaphoreType.DMA((2, PAIRS)),
            pltpu.SemaphoreType.DMA((2, PAIRS)),
            pltpu.SemaphoreType.DMA((2, n_sub - 1)),
            pltpu.SemaphoreType.DMA((2, n_sub - 1)),
        ],
        compiler_params=pltpu.CompilerParams(
            collective_id=0, has_side_effects=True, vmem_limit_bytes=56 * 1024 * 1024
        ),
        cost_estimate=pl.CostEstimate(
            flops=8_000_000_000, bytes_accessed=4_000_000, transcendentals=4_000_000
        ),
    )(
        initial_state,
        cotangent,
        volume_operator,
        in_weight.T,
        in_bias.reshape(1, -1),
        mid_weight,
        mid_bias.reshape(1, -1),
        out_weight,
        flux_matrix,
        dom_send,
        dom_count,
        sub_send,
        partner,
    )


def solution(mesh):
    return jax.shard_map(
        functools.partial(body, mesh.shape["dom"], mesh.shape["sub"]),
        mesh=mesh,
        in_specs=(
            P(None, ("dom", "sub")),
            P(None, ("dom", "sub")),
            P(),
            P(),
            P(),
            P(),
            P(),
            P(),
            P(),
            P("dom", "sub"),
            P("dom", "sub"),
            P("dom", "sub"),
            P("dom", "sub"),
        ),
        out_specs=(P(None, ("dom", "sub")), P(None, ("dom", "sub"))),
        check_vma=False,
    )
```
